256 devices in a mesh: cuts: 2 (over x_hi), fsdp: 128 (over y, x_lo, z, core).
Axes of the slice: x: 4 (x_hi: 2, x_lo: 2; x = x_hi * 2 + x_lo), y: 4, z: 8, core: 2. Of those that a mesh axis runs over, the one named last changes fastest.
Arguments:
- tokens: bfloat16 [98304, 8192], P(('cuts', 'fsdp')), may hold values from -33 to 33
- cotangent: bfloat16 [98304, 512], P(('cuts', 'fsdp')), may hold values from -0.022326078 to 0.022326078
- weight: float32 [8192, 512], P('fsdp'), may hold values from -17 to 17
- row_moment: float32 [8192], P('fsdp'), may hold values from 0.05 to 0.5
- col_moment: float32 [512], replicated, may hold values from 0.05 to 0.5
Outputs:
- new_weight: float32 [8192, 512], P('fsdp')
- delta: float32 [8192, 512], P('fsdp')
- rows_new: float32 [8192], P('fsdp')
- cols_new: float32 [512], replicated
- preact: bfloat16 [98304, 512], P(('cuts', 'fsdp'))
The draws below stay inside these ranges and needn't reach their ends.
All inputs are finite; a program needn't handle non-finite values.
Results may differ from the reference program's by a relative error of at most 0.0049.
Values may be sent and summed in bfloat16 or wider, within the bound.
No kernel may reach another device: no remote copies, remote signals or barrier semaphores. Data moves between devices by JAX's collectives and lax.ppermute only.
A program may use at most 128 MiB of HBM per device.

```python
import math
import jax
import jax.numpy as jnp
from jax import lax

D = 8192
FFS = 512
TOKENS = 98304


def rising(length):
    return 0.6 + 1.2 * jnp.arange(length, dtype=jnp.float32) / max(length - 1, 1)


def draw_tokens(key, part):
    key = jax.random.fold_in(key, 11)
    first, second = jax.random.split(key, 2)
    column_scale = jnp.exp(jax.random.uniform(second, (D,), jnp.float32, -0.7, 0.7)) * rising(D)
    base = jax.random.normal(first, (TOKENS, D), jnp.float32)
    base = jnp.clip(base, -5.0, 5.0)
    return (base * rising(TOKENS)[:, None] * column_scale[None, :]).astype(jnp.bfloat16)


def draw_cotangent(key, part):
    key = jax.random.fold_in(key, 23)
    first, second = jax.random.split(key, 2)
    column_scale = jnp.exp(jax.random.uniform(second, (FFS,), jnp.float32, -1.15, 1.15))
    base = jax.random.normal(first, (TOKENS, FFS), jnp.float32)
    base = jnp.clip(base, -5.0, 5.0)
    return (base * column_scale[None, :] * (0.4 / jnp.sqrt(jnp.float32(TOKENS)))).astype(jnp.bfloat16)


def draw_weight(key, part):
    key = jax.random.fold_in(key, 37)
    first, second = jax.random.split(key, 2)
    column_scale = jnp.exp(jax.random.uniform(second, (FFS,), jnp.float32, -0.6, 0.6))
    base = jnp.clip(jax.random.normal(first, (D, FFS), jnp.float32), -5.0, 5.0)
    return base * rising(D)[:, None] * column_scale[None, :]


def level_of(rng, shape, pieces, smallest, largest):
    factor_of = 1.0
    for position, blocks in pieces:
        draws = jax.random.uniform(jax.random.fold_in(jax.random.fold_in(rng, 6), position), (blocks,), jnp.float32, smallest / len(pieces), largest / len(pieces))
        factor_of = factor_of * jnp.repeat(jnp.exp(draws), shape[position] // blocks).reshape((-1,) + (1,) * (len(shape) - 1 - position))
    return factor_of


def setup_inputs(seed: int = 0) -> dict:
    seeds = jax.random.split(jax.random.key(seed), 6)
    tokens = draw_tokens(jax.random.fold_in(seeds[5], 71), 0)
    cotangent = draw_cotangent(jax.random.fold_in(seeds[5], 71), 0)
    weight = draw_weight(jax.random.fold_in(seeds[5], 71), 0)
    row_moment = jnp.clip(jnp.exp(math.log(0.5) - 2.3025851 * jax.random.uniform(seeds[3], (D,), jnp.float32) ** level_of(seeds[3], (D,), ((0, 128),), -0.2, 0.2)), 0.05, 0.5)
    col_moment = jnp.clip(jnp.exp(jax.random.uniform(seeds[4], (FFS,), jnp.float32, math.log(0.05), math.log(0.5))), 0.05, 0.5)
    return dict(tokens=tokens, cotangent=cotangent, weight=weight, row_moment=row_moment, col_moment=col_moment)


decay_rate = 0.9
tiny_square = 1e-30
clip_level = 1.0
weight_floor = 0.001
learn_rate = 0.1

def reference(tokens, cotangent, weight, row_moment, col_moment):
    gradient = jnp.dot(tokens.T, cotangent, preferred_element_type=jnp.float32)
    squares = gradient * gradient
    rows_new = decay_rate * row_moment + (1.0 - decay_rate) * (lax.optimization_barrier(jnp.mean(squares, axis=1)) + tiny_square)
    cols_new = decay_rate * col_moment + (1.0 - decay_rate) * (lax.optimization_barrier(jnp.mean(squares, axis=0)) + tiny_square)
    mean_row = jnp.sum(rows_new) / D
    update = gradient * jnp.sqrt(mean_row) * lax.rsqrt(rows_new)[:, None] * lax.rsqrt(cols_new)[None, :]
    update_rms = jnp.sqrt(jnp.mean(update * update))
    clipped = update / jnp.maximum(1.0, update_rms / clip_level)
    weight_rms = jnp.sqrt(jnp.mean(weight * weight))
    delta = jnp.maximum(weight_floor, weight_rms) * clipped
    new_weight = weight - learn_rate * delta
    half_weight = new_weight.astype(jnp.bfloat16)
    summed = jnp.dot(tokens, half_weight, preferred_element_type=jnp.float32)
    preact = (summed * (1.0 / jnp.sqrt(jnp.float32(D)))).astype(jnp.bfloat16)
    return (new_weight, delta, rows_new, cols_new, preact)
```

```python
import functools
import math

import jax
import jax.numpy as jnp
from jax import lax
from jax.experimental import pallas as pl
from jax.experimental.pallas import tpu as pltpu
from jax.sharding import Mesh, PartitionSpec as P

decay_rate = 0.9
tiny_square = 1e-30
clip_level = 1.0
weight_floor = 0.001
learn_rate = 0.1

f32 = jnp.float32
bf16 = jnp.bfloat16

AXES = ("cuts", "y1", "y0", "xlo", "z", "core")
SIZES = (2, 2, 2, 2, 8, 2)
Y = ("y1", "y0")
X = ("cuts", "xlo")
ZN = 8
GR = 16


def grad_kernel(pos, tok, tok2, cot, cot2, *outs):
    a_outs, b_outs = outs[:4], outs[4:]
    i, j = pl.program_id(0), pl.program_id(1)
    y1, cuts = pos[1], pos[4]
    dims = (((0,), (0,)), ((), ()))
    g = lax.dot_general(tok[...], cot[...], dims, preferred_element_type=f32)
    g = g + lax.dot_general(tok2[...], cot2[...], dims, preferred_element_type=f32)
    g = g.reshape(ZN, 2, 2, 2, GR, g.shape[-1])
    for rel in range(2):
        for other in range(2):
            a_val = jnp.where(y1 == 0, g[:, rel, other, 0], g[:, 1 - rel, other, 0])
            b_val = jnp.where(cuts == 0, g[:, other, rel, 1], g[:, other, 1 - rel, 1])
            for step in range(2):

                @pl.when(i == step)
                def _():
                    out = a_outs[rel * 2 + step]
                    out[j, other ^ cuts] = a_val.astype(out.dtype)

                @pl.when(j == step)
                def _():
                    out = b_outs[rel * 2 + step]
                    out[i, other ^ y1] = b_val.astype(out.dtype)


def apply_kernel(pos, tok, tok2, *refs):
    a_ins, b_ins, (own, away, half) = refs[:4], refs[4:8], refs[8:]
    i, j = pl.program_id(0), pl.program_id(1)
    y1, cuts = pos[1], pos[4]
    for step in range(2):
        for c in range(2):
            for r5 in range(2):

                @pl.when(i == step)
                def _():
                    r = r5 ^ cuts
                    half[:, c, r5, 0] = jnp.where(
                        y1 == 0, a_ins[c * 2 + step][j, r], a_ins[(1 - c) * 2 + step][j, r]
                    )

                @pl.when(j == step)
                def _():
                    r = c ^ y1
                    half[:, c, r5, 1] = jnp.where(
                        cuts == 0, b_ins[r5 * 2 + step][i, r], b_ins[(1 - r5) * 2 + step][i, r]
                    )

    h = half[...].reshape(-1, half.shape[-1])

    @pl.when((i == 0) & (j == 0))
    def _():
        own[...] = jnp.zeros_like(own)
        away[...] = jnp.zeros_like(away)

    own[...] += jnp.dot(tok[...], h, preferred_element_type=f32)
    away[...] += jnp.dot(tok2[...], h, preferred_element_type=f32)


def half_block(i, j, pos):
    return ((pos[2] ^ i) * 2) + (pos[3] ^ j)


def piece_spec(shape):
    return pl.BlockSpec(shape, lambda i, j, pos: (0,) * len(shape))


def xor_perm(n, k):
    return [(d, d ^ k) for d in range(n)]


SWAP = [(0, 1), (1, 0)]
TURN = [(0, 0), (1, 2), (2, 1), (3, 3)]


def exchange(pieces, axes):
    return [lax.ppermute(pieces[k], axes, xor_perm(4, k)) for k in (1, 2, 3)]


def four_sum(own, got):
    return (own + got[1]) + (got[0] + got[2])


def on_device(tokens, cotangent, weight, row_moment, col_moment):
    tok_rows, width = tokens.shape
    hidden = cotangent.shape[1]
    half_width = width // 2
    step_cols = half_width // 4
    cuts, y1, y0, xlo, _, core = [lax.axis_index(a) for a in AXES]
    pos = jnp.stack([core, y1, y0, xlo, cuts]).astype(jnp.int32)

    away_cols = lax.dynamic_slice_in_dim(tokens, (1 - core) * half_width, half_width, axis=1)
    tokens2 = lax.ppermute(away_cols, "core", SWAP)
    cotangent2 = lax.ppermute(cotangent, "core", SWAP)

    my_weight = lax.dynamic_slice_in_dim(weight, cuts * 32, 32, axis=0)
    my_moment = lax.dynamic_slice_in_dim(row_moment, cuts * 32, 32, axis=0)
    packed = jnp.concatenate(
        [my_weight, jnp.broadcast_to(my_moment[:, None], (32, 128))], axis=1
    )
    packed = lax.ppermute(packed, ("y1", "core"), TURN)
    w32 = packed[:, :hidden]
    moment32 = packed[:, hidden : hidden + 1]

    tok_specs = [
        pl.BlockSpec((tok_rows, step_cols), lambda i, j, pos: (0, pos[0] * 4 + half_block(i, j, pos))),
        pl.BlockSpec((tok_rows, step_cols), lambda i, j, pos: (0, half_block(i, j, pos))),
    ]
    piece = (2, 2, ZN, GR, hidden)
    kept, sent = jax.ShapeDtypeStruct(piece, f32), jax.ShapeDtypeStruct(piece, bf16)
    flops = 2 * 2 * tok_rows * half_width * hidden
    params = pltpu.CompilerParams(vmem_limit_bytes=48 * 2**20)
    cost = pl.CostEstimate(flops=flops, bytes_accessed=12 * 2**20, transcendentals=0)
    parts = pl.pallas_call(
        grad_kernel,
        out_shape=[kept, sent, sent, sent] * 2,
        grid_spec=pltpu.PrefetchScalarGridSpec(
            num_scalar_prefetch=1,
            grid=(2, 2),
            in_specs=tok_specs
            + [pl.BlockSpec((tok_rows, hidden), lambda i, j, pos: (0, 0))] * 2,
            out_specs=[piece_spec(piece)] * 8,
        ),
        compiler_params=params,
        cost_estimate=cost,
    )(pos, tokens, tokens2, cotangent, cotangent2)
    a_parts, b_parts = parts[:4], parts[4:]

    a_got, b_got = exchange(a_parts, Y), exchange(b_parts, X)
    a_sum = a_parts[0] + sum(p.astype(f32) for p in a_got)
    b_sum = b_parts[0] + sum(p.astype(f32) for p in b_got)

    a_parts = [a_sum[k % 2, k // 2] for k in range(4)]
    b_parts = [b_sum[k % 2, k // 2] for k in range(4)]
    a_got = exchange([p.astype(bf16) for p in a_parts], X)
    b_got = exchange([p.astype(bf16) for p in b_parts], Y)
    a_sum = a_parts[0] + sum(p.astype(f32) for p in a_got)
    b_sum = b_parts[0] + sum(p.astype(f32) for p in b_got)

    both = jnp.stack([a_sum, b_sum], axis=1).astype(bf16)
    g32 = jnp.sum(
        lax.all_to_all(both, "z", 0, 0, tiled=True).astype(f32), axis=0
    ).reshape(32, hidden)

    squares = g32 * g32
    rows32 = decay_rate * moment32 + (1.0 - decay_rate) * (
        jnp.mean(squares, axis=1, keepdims=True) + tiny_square
    )
    scaled = squares / rows32
    lane = lax.broadcasted_iota(jnp.int32, (1, hidden), 1)
    scalars = jnp.where(lane == 0, jnp.sum(rows32), 0.0) + jnp.where(
        lane == 1, jnp.sum(w32 * w32), 0.0
    )
    stats = jnp.concatenate(
        [jnp.sum(squares, axis=0, keepdims=True), jnp.sum(scaled, axis=0, keepdims=True), scalars],
        axis=0,
    )
    stats = stats + lax.ppermute(stats, "core", SWAP)
    stats = four_sum(stats, exchange([stats] * 4, Y))
    stats = four_sum(stats, exchange([stats] * 4, X))
    stats = four_sum(stats, [lax.ppermute(stats, "z", xor_perm(8, k)) for k in (1, 2, 3)])
    stats = stats + lax.ppermute(stats, "z", xor_perm(8, 4))
    col_total, scaled_total, row_total, weight_total = stats[0], stats[1], stats[2, 0], stats[2, 1]

    cols_new = decay_rate * col_moment + (1.0 - decay_rate) * (col_total / width + tiny_square)
    mean_row = row_total / width
    update_total = mean_row * jnp.sum(scaled_total / cols_new)
    update_rms = jnp.sqrt(update_total / (width * hidden))
    weight_rms = jnp.sqrt(weight_total / (width * hidden))
    factor = (
        jnp.sqrt(mean_row)
        * jnp.maximum(weight_floor, weight_rms)
        / jnp.maximum(1.0, update_rms / clip_level)
    )
    inv_cols = factor * lax.rsqrt(cols_new)[None, :]
    half32 = (w32 - learn_rate * (g32 * lax.rsqrt(rows32) * inv_cols)).astype(bf16)

    half_z = lax.all_to_all(
        jnp.broadcast_to(half32[None], (ZN, 32, hidden)), "z", 0, 0, tiled=True
    ).reshape(ZN, 2, GR, hidden)
    a_half, b_half = half_z[:, 0], half_z[:, 1]
    a_all = [a_half] + exchange([a_half] * 4, X)
    b_all = [b_half] + exchange([b_half] * 4, Y)
    a_half = jnp.stack([a_all[0], a_all[2], a_all[1], a_all[3]]).reshape(piece)
    b_half = jnp.stack([b_all[0], b_all[2], b_all[1], b_all[3]]).reshape(piece)
    a_all = [a_half] + exchange([a_half] * 4, Y)
    b_all = [b_half] + exchange([b_half] * 4, X)

    result = jax.ShapeDtypeStruct((tok_rows, hidden), f32)
    own, away = pl.pallas_call(
        apply_kernel,
        out_shape=[result, result],
        grid_spec=pltpu.PrefetchScalarGridSpec(
            num_scalar_prefetch=1,
            grid=(2, 2),
            in_specs=tok_specs + [piece_spec(piece)] * 8,
            out_specs=[pl.BlockSpec((tok_rows, hidden), lambda i, j, pos: (0, 0))] * 2,
            scratch_shapes=[pltpu.VMEM((ZN, 2, 2, 2, GR, hidden), bf16)],
        ),
        compiler_params=params,
        cost_estimate=cost,
    )(pos, tokens, tokens2, *a_all, *b_all)
    summed = own + lax.ppermute(away, "core", SWAP)
    preact = (summed * (1.0 / math.sqrt(width))).astype(bf16)

    near = lax.ppermute(g32, ("y1", "core"), TURN)
    far = lax.ppermute(near, "cuts", SWAP)
    g64 = jnp.where(
        cuts == 0, jnp.concatenate([near, far], axis=0), jnp.concatenate([far, near], axis=0)
    )
    rows_new = decay_rate * row_moment + (1.0 - decay_rate) * (
        jnp.mean(g64 * g64, axis=1) + tiny_square
    )
    delta = g64 * lax.rsqrt(rows_new)[:, None] * inv_cols
    new_weight = weight - learn_rate * delta
    return (new_weight, delta, rows_new, cols_new, preact)


def solution(mesh):
    fine = Mesh(mesh.devices.reshape(SIZES), AXES)
    fsdp = ("y1", "y0", "xlo", "z", "core")
    rows = P(("cuts",) + fsdp, None)
    return jax.shard_map(
        on_device,
        mesh=fine,
        in_specs=(rows, rows, P(fsdp, None), P(fsdp), P()),
        out_specs=(P(fsdp, None), P(fsdp, None), P(fsdp), P(), rows),
        check_vma=False,
    )
```

```python
import functools
import math

import jax
import jax.numpy as jnp
from jax import lax
from jax.experimental import pallas as pl
from jax.experimental.pallas import tpu as pltpu
from jax.sharding import Mesh, PartitionSpec as P

decay_rate = 0.9
tiny_square = 1e-30
clip_level = 1.0
weight_floor = 0.001
learn_rate = 0.1

f32 = jnp.float32
bf16 = jnp.bfloat16

AXES = ("cuts", "y1", "y0", "xlo", "z", "core")
SIZES = (2, 2, 2, 2, 8, 2)
Y = ("y1", "y0")
X = ("cuts", "xlo")
ZN = 8
ZH = 4
GR = 32
SWAP = [(0, 1), (1, 0)]
TURN = [(0, 0), (1, 2), (2, 1), (3, 3)]
FAR_TURN = [(d + 4 * q, e + 4 * (1 - q)) for q in range(2) for d, e in TURN]


def cols_at(part, step):
    def index(g, pos):
        row_bit, x_bit = (step, g) if part == 0 else (g, step)
        return (pos[2] ^ row_bit) * 4 + (pos[3] ^ x_bit) * 2 + part

    return index


def chosen(pos, part):
    return (pos[1], pos[4]) if part == 0 else (pos[4], pos[1])


def copy_kernel(pos, src, dst):
    dst[...] = src[...]


def grad_kernel(part, pos, tok, tok2, cot, cot2, out0, out1):
    pick, inner = chosen(pos, part)
    dims = (((0,), (0,)), ((), ()))
    g = lax.dot_general(tok[...], cot[...], dims, preferred_element_type=f32)
    g = g + lax.dot_general(tok2[...], cot2[...], dims, preferred_element_type=f32)
    g = g.reshape(ZH, 2, 2, GR, g.shape[-1])
    for k in range(2):
        first, second = (g[:, 0, k], g[:, 1, k]) if part == 0 else (g[:, k, 0], g[:, k, 1])
        out0[0, k ^ inner] = jnp.where(pick == 0, first, second).astype(out0.dtype)
        out1[0, k ^ inner] = jnp.where(pick == 0, second, first).astype(out1.dtype)


def apply_kernel(part, n_after, pos, tok, tok2, piece0, piece1, *refs):
    refs = refs[n_after:]
    sums, (own, away, half) = refs[:-3], refs[-3:]
    pick, inner = chosen(pos, part)
    for k in range(2):
        zero, one = piece0[0, k ^ inner], piece1[0, k ^ inner]
        first, second = jnp.where(pick == 0, zero, one), jnp.where(pick == 0, one, zero)
        if part == 0:
            half[:, 0, k], half[:, 1, k] = first, second
        else:
            half[:, k, 0], half[:, k, 1] = first, second
    h = half[...].reshape(-1, half.shape[-1])

    @pl.when(pl.program_id(0) == 0)
    def _():
        for out, begin in zip((own, away), sums or (None, None)):
            out[...] = jnp.zeros_like(out) if begin is None else begin[...]

    own[...] += jnp.dot(tok[...], h, preferred_element_type=f32)
    away[...] += jnp.dot(tok2[...], h, preferred_element_type=f32)


def xor_perm(n, k):
    return [(d, d ^ k) for d in range(n)]


def exchange(pieces, axes):
    return [lax.ppermute(pieces[k], axes, xor_perm(4, k)) for k in (1, 2, 3)]


def four_sum(own, got):
    return (own + got[1]) + (got[0] + got[2])


def on_device(tokens, cotangent, weight, row_moment, col_moment):
    tok_rows, width = tokens.shape
    hidden = cotangent.shape[1]
    seg = width // 16
    cuts, y1, y0, xlo, _, core = [lax.axis_index(a) for a in AXES]
    pos = jnp.stack([core, y1, y0, xlo, cuts]).astype(jnp.int32)
    params = pltpu.CompilerParams(vmem_limit_bytes=32 * 2**20)
    cost = pl.CostEstimate(
        flops=4 * tok_rows * 2 * seg * hidden, bytes_accessed=4 * 2**20, transcendentals=0
    )
    piece = (2, 2, ZH, GR, hidden)
    whole = pl.BlockSpec((tok_rows, hidden), lambda g, pos: (0, 0))
    piece_spec = pl.BlockSpec((1,) + piece[1:], lambda g, pos: (g, 0, 0, 0, 0))

    def tok_specs(part, step):
        index = cols_at(part, step)
        return [
            pl.BlockSpec((tok_rows, seg), lambda g, pos: (0, pos[0] * 8 + index(g, pos))),
            pl.BlockSpec((tok_rows, seg), lambda g, pos: (0, g)),
        ]

    order = [(0, 1), (1, 1), (0, 0), (1, 0)]
    cotangent2 = lax.ppermute(cotangent, "core", SWAP)
    tokens2 = {}
    for part, step in order:
        index = cols_at(part, step)
        away_cols = pl.pallas_call(
            copy_kernel,
            out_shape=jax.ShapeDtypeStruct((tok_rows, 2 * seg), tokens.dtype),
            grid_spec=pltpu.PrefetchScalarGridSpec(
                num_scalar_prefetch=1,
                grid=(2,),
                in_specs=[
                    pl.BlockSpec(
                        (tok_rows, seg),
                        lambda g, pos, index=index: (0, (1 - pos[0]) * 8 + index(g, pos)),
                    )
                ],
                out_specs=pl.BlockSpec((tok_rows, seg), lambda g, pos: (0, g)),
            ),
            compiler_params=params,
        )(pos, tokens)
        tokens2[part, step] = lax.ppermute(away_cols, "core", SWAP)

    my_weight = lax.dynamic_slice_in_dim(weight, cuts * 32, 32, axis=0)
    my_moment = lax.dynamic_slice_in_dim(row_moment, cuts * 32, 32, axis=0)
    packed = jnp.concatenate(
        [my_weight, jnp.broadcast_to(my_moment[:, None], (32, 128))], axis=1
    )
    packed = lax.ppermute(packed, ("y1", "core"), TURN)
    packed = lax.all_gather(packed, "z", axis=0, tiled=True)

    parts = {}
    for part, step in order:
        kept = jax.ShapeDtypeStruct(piece, bf16 if step else f32)
        parts[part, step], parts[part, 2 + step] = pl.pallas_call(
            functools.partial(grad_kernel, part),
            out_shape=[kept, jax.ShapeDtypeStruct(piece, bf16)],
            grid_spec=pltpu.PrefetchScalarGridSpec(
                num_scalar_prefetch=1,
                grid=(2,),
                in_specs=tok_specs(part, step) + [whole] * 2,
                out_specs=[piece_spec] * 2,
            ),
            compiler_params=params,
            cost_estimate=cost,
        )(pos, tokens, tokens2[part, step], cotangent, cotangent2)

    a_parts, b_parts = [[parts[p, k] for k in range(4)] for p in range(2)]
    a_got, b_got = exchange(a_parts, Y), exchange(b_parts, X)
    a_sum = a_parts[0] + sum(p.astype(f32) for p in a_got)
    b_sum = b_parts[0] + sum(p.astype(f32) for p in b_got)

    a_parts = [a_sum[k % 2, k // 2] for k in range(4)]
    b_parts = [b_sum[k % 2, k // 2] for k in range(4)]
    a_got = exchange([p.astype(bf16) for p in a_parts], X)
    b_got = exchange([p.astype(bf16) for p in b_parts], Y)
    a_sum = a_parts[0] + sum(p.astype(f32) for p in a_got)
    b_sum = b_parts[0] + sum(p.astype(f32) for p in b_got)

    both = jnp.concatenate([a_sum, b_sum], axis=0).astype(bf16)
    g32 = jnp.sum(lax.all_to_all(both, "z", 0, 0, tiled=True).astype(f32), axis=0)

    near = lax.ppermute(g32, ("y1", "core"), TURN)
    far = lax.ppermute(g32, ("cuts", "y1", "core"), FAR_TURN)

    gz = lax.all_to_all(
        jnp.broadcast_to(g32.astype(bf16)[None], (ZN, GR, hidden)), "z", 0, 0, tiled=True
    )
    gz, packed, near, far = lax.optimization_barrier((gz, packed, near, far))
    gz = gz.reshape(ZN * GR, hidden).astype(f32)
    wz = packed[:, :hidden]
    moment_z = packed[:, hidden : hidden + 1]

    squares = gz * gz
    rows_z = decay_rate * moment_z + (1.0 - decay_rate) * (
        jnp.mean(squares, axis=1, keepdims=True) + tiny_square
    )
    lane = lax.broadcasted_iota(jnp.int32, (1, hidden), 1)
    scalars = jnp.where(lane == 0, jnp.sum(rows_z), 0.0) + jnp.where(
        lane == 1, jnp.sum(wz * wz), 0.0
    )
    stats = jnp.concatenate(
        [
            jnp.sum(squares, axis=0, keepdims=True),
            jnp.sum(squares / rows_z, axis=0, keepdims=True),
            scalars,
        ],
        axis=0,
    )
    stats = stats + lax.ppermute(stats, "core", SWAP)
    stats = four_sum(stats, exchange([stats] * 4, Y))
    stats = four_sum(stats, exchange([stats] * 4, X))
    col_total, scaled_total, row_total, weight_total = stats[0], stats[1], stats[2, 0], stats[2, 1]

    cols_new = decay_rate * col_moment + (1.0 - decay_rate) * (col_total / width + tiny_square)
    mean_row = row_total / width
    update_total = mean_row * jnp.sum(scaled_total / cols_new)
    update_rms = jnp.sqrt(update_total / (width * hidden))
    weight_rms = jnp.sqrt(weight_total / (width * hidden))
    factor = (
        jnp.sqrt(mean_row)
        * jnp.maximum(weight_floor, weight_rms)
        / jnp.maximum(1.0, update_rms / clip_level)
    )
    inv_cols = factor * lax.rsqrt(cols_new)[None, :]
    half_z = (wz - learn_rate * (gz * lax.rsqrt(rows_z) * inv_cols)).astype(bf16)
    half_z = half_z.reshape(2, ZH, GR, hidden)

    a_half, b_half = half_z[0], half_z[1]
    a_all = [a_half] + exchange([a_half] * 4, X)
    b_all = [b_half] + exchange([b_half] * 4, Y)
    a_half = jnp.stack([a_all[0], a_all[2], a_all[1], a_all[3]]).reshape(piece)
    b_half = jnp.stack([b_all[0], b_all[2], b_all[1], b_all[3]]).reshape(piece)
    a_half, b_half = lax.optimization_barrier((a_half, b_half))
    a_all = [a_half] + exchange([a_half] * 4, Y)
    b_all = [b_half] + exchange([b_half] * 4, X)

    g64 = jnp.where(
        cuts == 0, jnp.concatenate([near, far], axis=0), jnp.concatenate([far, near], axis=0)
    )
    rows_new = decay_rate * row_moment + (1.0 - decay_rate) * (
        jnp.mean(g64 * g64, axis=1) + tiny_square
    )
    delta = g64 * lax.rsqrt(rows_new)[:, None] * inv_cols
    new_weight = weight - learn_rate * delta

    result = jax.ShapeDtypeStruct((tok_rows, hidden), f32)
    sums = []
    for part, step in [(0, 0), (1, 0), (0, 1), (1, 1)]:
        halves = (a_all, b_all)[part]
        after = [new_weight] if (part, step) == (1, 0) else []
        sums = pl.pallas_call(
            functools.partial(apply_kernel, part, len(after)),
            out_shape=[result, result],
            grid_spec=pltpu.PrefetchScalarGridSpec(
                num_scalar_prefetch=1,
                grid=(2,),
                in_specs=tok_specs(part, step)
                + [piece_spec] * 2
                + [pl.BlockSpec(memory_space=pl.ANY)] * len(after)
                + [whole] * len(sums),
                out_specs=[whole] * 2,
                scratch_shapes=[pltpu.VMEM((ZH, 2, 2, GR, hidden), bf16)],
            ),
            compiler_params=params,
            cost_estimate=cost,
        )(pos, tokens, tokens2[part, step], halves[step], halves[2 + step], *after, *sums)
    own, away = sums
    summed = own + lax.ppermute(away, "core", SWAP)
    preact = (summed * (1.0 / math.sqrt(width))).astype(bf16)
    return (new_weight, delta, rows_new, cols_new, preact)


def solution(mesh):
    fine = Mesh(mesh.devices.reshape(SIZES), AXES)
    fsdp = ("y1", "y0", "xlo", "z", "core")
    rows = P(("cuts",) + fsdp, None)
    return jax.shard_map(
        on_device,
        mesh=fine,
        in_specs=(rows, rows, P(fsdp, None), P(fsdp), P()),
        out_specs=(P(fsdp, None), P(fsdp, None), P(fsdp), P(), rows),
        check_vma=False,
    )
```

```python
import functools
import math

import jax
import jax.numpy as jnp
from jax import lax
from jax.experimental import pallas as pl
from jax.experimental.pallas import tpu as pltpu
from jax.sharding import Mesh, PartitionSpec as P

decay_rate = 0.9
tiny_square = 1e-30
clip_level = 1.0
weight_floor = 0.001
learn_rate = 0.1

f32 = jnp.float32
bf16 = jnp.bfloat16

AXES = ("cuts", "y1", "y0", "xlo", "z", "core")
SIZES = (2, 2, 2, 2, 8, 2)
Y = ("y1", "y0")
X = ("cuts", "xlo")
ZN = 8
ZH = 4
GR = 32
SWAP = [(0, 1), (1, 0)]
TURN = [(0, 0), (1, 2), (2, 1), (3, 3)]
FAR_TURN = [(d + 4 * q, e + 4 * (1 - q)) for q in range(2) for d, e in TURN]


def cols_at(part, step):
    def index(g, pos):
        row_bit, x_bit = (step, g) if part == 0 else (g, step)
        return (pos[2] ^ row_bit) * 4 + (pos[3] ^ x_bit) * 2 + part

    return index


def chosen(pos, part):
    return (pos[1], pos[4]) if part == 0 else (pos[4], pos[1])


def copy_kernel(pos, src, dst):
    dst[...] = src[...]


def grad_kernel(part, pos, tok, tok2, cot, cot2, out0, out1):
    pick, inner = chosen(pos, part)
    dims = (((0,), (0,)), ((), ()))
    g = lax.dot_general(tok[...], cot[...], dims, preferred_element_type=f32)
    g = g + lax.dot_general(tok2[...], cot2[...], dims, preferred_element_type=f32)
    g = g.reshape(ZH, 2, 2, GR, g.shape[-1])
    for k in range(2):
        first, second = (g[:, 0, k], g[:, 1, k]) if part == 0 else (g[:, k, 0], g[:, k, 1])
        out0[0, k ^ inner] = jnp.where(pick == 0, first, second).astype(out0.dtype)
        out1[0, k ^ inner] = jnp.where(pick == 0, second, first).astype(out1.dtype)


def apply_kernel(part, pos, tok, tok2, piece0, piece1, *refs):
    sums, (own, away, half) = refs[:-3], refs[-3:]
    pick, inner = chosen(pos, part)
    for k in range(2):
        zero, one = piece0[0, k ^ inner], piece1[0, k ^ inner]
        first, second = jnp.where(pick == 0, zero, one), jnp.where(pick == 0, one, zero)
        if part == 0:
            half[:, 0, k], half[:, 1, k] = first, second
        else:
            half[:, k, 0], half[:, k, 1] = first, second
    h = half[...].reshape(-1, half.shape[-1])

    @pl.when(pl.program_id(0) == 0)
    def _():
        for out, begin in zip((own, away), sums or (None, None)):
            out[...] = jnp.zeros_like(out) if begin is None else begin[...]

    own[...] += jnp.dot(tok[...], h, preferred_element_type=f32)
    away[...] += jnp.dot(tok2[...], h, preferred_element_type=f32)


def second_sum_kernel(*refs):
    out = refs[-1]
    for part in range(2):
        own, first, second, third = refs[4 * part : 4 * part + 4]
        total = own[...] + first[...].astype(f32) + second[...].astype(f32)
        out[ZH * part : ZH * part + ZH] = (total + third[...].astype(f32)).astype(out.dtype)


def row_moment_of(moment, squares):
    mean = jnp.sum(squares, axis=1, keepdims=True) * (1.0 / squares.shape[1])
    return decay_rate * moment + (1.0 - decay_rate) * (mean + tiny_square)


def stats_kernel(gz, packed, stats, scaled):
    hidden = gz.shape[-1]
    cols = jnp.zeros((GR, hidden), f32)
    scaled_cols = jnp.zeros((GR, hidden), f32)
    weights = jnp.zeros((GR, hidden), f32)
    row_total = jnp.zeros((GR, 1), f32)
    for z in range(ZN):
        g = gz[z].astype(f32)
        squares = g * g
        rows = row_moment_of(packed[z, :, hidden : hidden + 1], squares)
        u = g * lax.rsqrt(rows)
        scaled[z] = u
        w = packed[z, :, :hidden]
        cols, scaled_cols, weights = cols + squares, scaled_cols + u * u, weights + w * w
        row_total = row_total + rows
    lane = lax.broadcasted_iota(jnp.int32, (1, hidden), 1)
    total = lambda v: jnp.sum(v, axis=0, keepdims=True)
    scalars = jnp.where(lane == 0, total(row_total), 0.0) + jnp.where(
        lane == 1, jnp.sum(total(weights), axis=1, keepdims=True), 0.0
    )
    stats[...] = jnp.zeros_like(stats)
    stats[0:1], stats[1:2], stats[2:3] = total(cols), total(scaled_cols), scalars


def rows_kernel(width, stats, col_moment, packed, scaled, a_half, b_half, cols_new, inv_cols):
    hidden = scaled.shape[-1]
    lane = lax.broadcasted_iota(jnp.int32, (1, hidden), 1)
    pick = lambda k: jnp.sum(jnp.where(lane == k, stats[2:3], 0.0), axis=1, keepdims=True)
    cols = decay_rate * col_moment[...] + (1.0 - decay_rate) * (
        stats[0:1] * (1.0 / width) + tiny_square
    )
    mean_row = pick(0) * (1.0 / width)
    update_total = mean_row * jnp.sum(stats[1:2] / cols, axis=1, keepdims=True)
    update_rms = jnp.sqrt(update_total * (1.0 / (width * hidden)))
    weight_rms = jnp.sqrt(pick(1) * (1.0 / (width * hidden)))
    factor = (
        jnp.sqrt(mean_row)
        * jnp.maximum(weight_floor, weight_rms)
        / jnp.maximum(1.0, update_rms / clip_level)
    )
    inv = factor * lax.rsqrt(cols)
    cols_new[...], inv_cols[...] = cols, inv
    for z in range(ZN):
        new = packed[z, :, :hidden] - learn_rate * (scaled[z] * inv)
        (a_half, b_half)[z // ZH][z % ZH] = new.astype(bf16)


def return_kernel(pos, near, far, weight, moment, inv_cols, new_weight, delta, rows_new):
    for k, source in enumerate((near, far)):
        rows = pl.ds(pl.multiple_of(GR * (k ^ pos[4]), GR), GR)
        g = source[...]
        moments = row_moment_of(moment[rows], g * g)
        change = g * lax.rsqrt(moments) * inv_cols[...]
        rows_new[rows] = moments
        delta[rows] = change
        new_weight[rows] = weight[rows] - learn_rate * change


def xor_perm(n, k):
    return [(d, d ^ k) for d in range(n)]


def exchange(pieces, axes):
    return [lax.ppermute(pieces[k], axes, xor_perm(4, k)) for k in (1, 2, 3)]


def four_sum(own, got):
    return (own + got[1]) + (got[0] + got[2])


def on_device(tokens, cotangent, weight, row_moment, col_moment):
    tok_rows, width = tokens.shape
    hidden = cotangent.shape[1]
    seg = width // 16
    cuts, y1, y0, xlo, _, core = [lax.axis_index(a) for a in AXES]
    pos = jnp.stack([core, y1, y0, xlo, cuts]).astype(jnp.int32)
    params = pltpu.CompilerParams(vmem_limit_bytes=32 * 2**20)
    cost = pl.CostEstimate(
        flops=4 * tok_rows * 2 * seg * hidden, bytes_accessed=4 * 2**20, transcendentals=0
    )
    piece = (2, 2, ZH, GR, hidden)
    whole = pl.BlockSpec((tok_rows, hidden), lambda g, pos: (0, 0))
    piece_spec = pl.BlockSpec((1,) + piece[1:], lambda g, pos: (g, 0, 0, 0, 0))

    def tok_specs(part, step):
        index = cols_at(part, step)
        return [
            pl.BlockSpec((tok_rows, seg), lambda g, pos: (0, pos[0] * 8 + index(g, pos))),
            pl.BlockSpec((tok_rows, seg), lambda g, pos: (0, g)),
        ]

    order = [(0, 0), (1, 0), (0, 1), (1, 1)]
    cotangent2 = lax.ppermute(cotangent, "core", SWAP)
    tokens2 = {}
    for part, step in order:
        index = cols_at(part, step)
        away_cols = pl.pallas_call(
            copy_kernel,
            out_shape=jax.ShapeDtypeStruct((tok_rows, 2 * seg), tokens.dtype),
            grid_spec=pltpu.PrefetchScalarGridSpec(
                num_scalar_prefetch=1,
                grid=(2,),
                in_specs=[
                    pl.BlockSpec(
                        (tok_rows, seg),
                        lambda g, pos, index=index: (0, (1 - pos[0]) * 8 + index(g, pos)),
                    )
                ],
                out_specs=pl.BlockSpec((tok_rows, seg), lambda g, pos: (0, g)),
            ),
            compiler_params=params,
        )(pos, tokens)
        tokens2[part, step] = lax.ppermute(away_cols, "core", SWAP)

    my_weight = lax.dynamic_slice_in_dim(weight, cuts * 32, 32, axis=0)
    my_moment = lax.dynamic_slice_in_dim(row_moment, cuts * 32, 32, axis=0)
    packed = jnp.concatenate(
        [my_weight, jnp.broadcast_to(my_moment[:, None], (32, 128))], axis=1
    )
    packed = lax.ppermute(packed, ("y1", "core"), TURN)

    tokens2, cotangent2 = lax.optimization_barrier((tokens2, cotangent2))
    parts, chain = {}, pos
    for part, step in order:
        kept = jax.ShapeDtypeStruct(piece, bf16 if step else f32)
        parts[part, step], parts[part, 2 + step] = pl.pallas_call(
            functools.partial(grad_kernel, part),
            out_shape=[kept, jax.ShapeDtypeStruct(piece, bf16)],
            grid_spec=pltpu.PrefetchScalarGridSpec(
                num_scalar_prefetch=1,
                grid=(2,),
                in_specs=tok_specs(part, step) + [whole] * 2,
                out_specs=[piece_spec] * 2,
            ),
            compiler_params=params,
            cost_estimate=cost,
        )(chain, tokens, tokens2[part, step], cotangent, cotangent2)
        chain, _ = lax.optimization_barrier((pos, parts[part, 2 + step]))
    packed, parts[1, 3] = lax.optimization_barrier((packed, parts[1, 3]))
    packed = lax.all_to_all(
        jnp.broadcast_to(packed[None], (ZN,) + packed.shape), "z", 0, 0, tiled=True
    )

    a_parts, b_parts = [[parts[p, k] for k in range(4)] for p in range(2)]
    a_got, b_got = exchange(a_parts, Y), exchange(b_parts, X)
    a_sum = a_parts[0] + sum(p.astype(f32) for p in a_got)
    b_sum = b_parts[0] + sum(p.astype(f32) for p in b_got)

    a_parts = [a_sum[k % 2, k // 2] for k in range(4)]
    b_parts = [b_sum[k % 2, k // 2] for k in range(4)]
    a_got = exchange([p.astype(bf16) for p in a_parts], X)
    b_got = exchange([p.astype(bf16) for p in b_parts], Y)
    b_got, packed = lax.optimization_barrier((b_got, packed))
    line = (ZN, GR, hidden)
    both = pl.pallas_call(
        second_sum_kernel, out_shape=jax.ShapeDtypeStruct(line, bf16), compiler_params=params
    )(a_parts[0], *a_got, b_parts[0], *b_got)

    g32 = jnp.sum(lax.all_to_all(both, "z", 0, 0, tiled=True).astype(f32), axis=0)

    near = lax.ppermute(g32, ("y1", "core"), TURN)
    far = lax.ppermute(g32, ("cuts", "y1", "core"), FAR_TURN)

    gz = lax.all_to_all(jnp.broadcast_to(g32.astype(bf16)[None], line), "z", 0, 0, tiled=True)
    gz, near, far = lax.optimization_barrier((gz, near, far))

    stats, scaled = pl.pallas_call(
        stats_kernel,
        out_shape=[jax.ShapeDtypeStruct((8, hidden), f32), jax.ShapeDtypeStruct(line, f32)],
        compiler_params=params,
    )(gz, packed)
    stats = stats + lax.ppermute(stats, "core", SWAP)
    stats = four_sum(stats, exchange([stats] * 4, Y))
    stats = four_sum(stats, exchange([stats] * 4, X))

    row_vector = jax.ShapeDtypeStruct((1, hidden), f32)
    a_half, b_half, cols_new, inv_cols = pl.pallas_call(
        functools.partial(rows_kernel, width),
        out_shape=[jax.ShapeDtypeStruct((ZH, GR, hidden), bf16)] * 2 + [row_vector] * 2,
        compiler_params=params,
    )(stats, col_moment.reshape(1, hidden), packed, scaled)
    a_all = [a_half] + exchange([a_half] * 4, X)
    b_all = [b_half] + exchange([b_half] * 4, Y)
    a_half = jnp.stack([a_all[0], a_all[2], a_all[1], a_all[3]]).reshape(piece)
    b_half = jnp.stack([b_all[0], b_all[2], b_all[1], b_all[3]]).reshape(piece)
    a_half, b_half = lax.optimization_barrier((a_half, b_half))
    a_all, b_all = [a_half], [b_half]
    got = {}
    for k in (2, 1, 3):
        got[0, k] = lax.ppermute(a_half, Y, xor_perm(4, k))
        got[1, k] = lax.ppermute(b_half, X, xor_perm(4, k))
    a_all += [got[0, k] for k in (1, 2, 3)]
    b_all += [got[1, k] for k in (1, 2, 3)]

    slab = jax.ShapeDtypeStruct(weight.shape, f32)
    new_weight, delta, rows_new = pl.pallas_call(
        return_kernel,
        out_shape=[slab, slab, jax.ShapeDtypeStruct((weight.shape[0], 1), f32)],
        in_specs=[pl.BlockSpec(memory_space=pltpu.SMEM)]
        + [pl.BlockSpec(memory_space=pltpu.VMEM)] * 5,
        compiler_params=params,
    )(pos, near, far, weight, row_moment[:, None], inv_cols)
    a_all[2], _ = lax.optimization_barrier((a_all[2], rows_new))

    result = jax.ShapeDtypeStruct((tok_rows, hidden), f32)
    sums = []
    for part, step in [(0, 0), (1, 0), (0, 1), (1, 1)]:
        halves = (a_all, b_all)[part]
        sums = pl.pallas_call(
            functools.partial(apply_kernel, part),
            out_shape=[result, result],
            grid_spec=pltpu.PrefetchScalarGridSpec(
                num_scalar_prefetch=1,
                grid=(2,),
                in_specs=tok_specs(part, step)
                + [piece_spec] * 2
                + [whole] * len(sums),
                out_specs=[whole] * 2,
                scratch_shapes=[pltpu.VMEM((ZH, 2, 2, GR, hidden), bf16)],
            ),
            compiler_params=params,
            cost_estimate=cost,
        )(pos, tokens, tokens2[part, step], halves[step], halves[2 + step], *sums)
    own, away = sums
    summed = own + lax.ppermute(away, "core", SWAP)
    preact = (summed * (1.0 / math.sqrt(width))).astype(bf16)
    return (new_weight, delta, rows_new[:, 0], cols_new[0], preact)


def solution(mesh):
    fine = Mesh(mesh.devices.reshape(SIZES), AXES)
    fsdp = ("y1", "y0", "xlo", "z", "core")
    rows = P(("cuts",) + fsdp, None)
    return jax.shard_map(
        on_device,
        mesh=fine,
        in_specs=(rows, rows, P(fsdp, None), P(fsdp), P()),
        out_specs=(P(fsdp, None), P(fsdp, None), P(fsdp), P(), rows),
        check_vma=False,
    )
```

```python
import functools
import math

import jax
import jax.numpy as jnp
from jax import lax
from jax.experimental import pallas as pl
from jax.experimental.pallas import tpu as pltpu
from jax.sharding import Mesh, PartitionSpec as P

decay_rate = 0.9
tiny_square = 1e-30
clip_level = 1.0
weight_floor = 0.001
learn_rate = 0.1

f32 = jnp.float32
bf16 = jnp.bfloat16

AXES = ("cuts", "y1", "y0", "xlo", "z", "core")
SIZES = (2, 2, 2, 2, 8, 2)
Y = ("y1", "y0")
X = ("cuts", "xlo")
ZN = 8
ZH = 4
GR = 32
SWAP = [(0, 1), (1, 0)]


def reverse_bits(z):
    return (z & 1) * 4 + (z & 2) + (z // 4)


TURN = [
    ((y * ZN + z) * 2 + c, (c * ZN + reverse_bits(z)) * 2 + y)
    for y in range(2)
    for z in range(ZN)
    for c in range(2)
]
FAR_TURN = [(d + 32 * q, e + 32 * (1 - q)) for q in range(2) for d, e in TURN]
TURNED = ("y1", "z", "core")
LINE_STEP = {1: 4, 2: 2, 3: 6}


def cols_at(part, step):
    def index(g, pos):
        row_bit, x_bit = (step, g) if part == 0 else (g, step)
        return (pos[2] ^ row_bit) * 4 + (pos[3] ^ x_bit) * 2 + part

    return index


def chosen(pos, part):
    return (pos[1], pos[4]) if part == 0 else (pos[4], pos[1])


def copy_kernel(pos, src, dst):
    dst[...] = src[...]


def grad_kernel(part, pos, tok, tok2, cot, cot2, out0, out1):
    pick, inner = chosen(pos, part)
    dims = (((0,), (0,)), ((), ()))
    g = lax.dot_general(tok[...], cot[...], dims, preferred_element_type=f32)
    g = g + lax.dot_general(tok2[...], cot2[...], dims, preferred_element_type=f32)
    g = g.reshape(ZH, 2, 2, GR, g.shape[-1])
    for k in range(2):
        first, second = (g[:, 0, k], g[:, 1, k]) if part == 0 else (g[:, k, 0], g[:, k, 1])
        out0[0, k ^ inner] = jnp.where(pick == 0, first, second).astype(out0.dtype)
        out1[0, k ^ inner] = jnp.where(pick == 0, second, first).astype(out1.dtype)


def apply_kernel(part, pos, tok, tok2, piece0, piece1, *refs):
    sums, (own, away, half) = refs[:-3], refs[-3:]
    pick, inner = chosen(pos, part)
    for k in range(2):
        zero, one = piece0[0, k ^ inner], piece1[0, k ^ inner]
        first, second = jnp.where(pick == 0, zero, one), jnp.where(pick == 0, one, zero)
        if part == 0:
            half[:, 0, k], half[:, 1, k] = first, second
        else:
            half[:, k, 0], half[:, k, 1] = first, second
    h = half[...].reshape(-1, half.shape[-1])

    @pl.when(pl.program_id(0) == 0)
    def _():
        for out, begin in zip((own, away), sums or (None, None)):
            out[...] = jnp.zeros_like(out) if begin is None else begin[...]

    own[...] += jnp.dot(tok[...], h, preferred_element_type=f32)
    away[...] += jnp.dot(tok2[...], h, preferred_element_type=f32)


def second_sum_kernel(pos, *refs):
    ins, (keep, send) = refs[:8], refs[8:]
    a_sum, b_sum = [
        ins[n][...] + sum(ins[n + k][...].astype(f32) for k in (1, 2, 3)) for n in (0, 4)
    ]
    upper = pos[5] >= ZH
    keep[...] = jnp.where(upper, b_sum, a_sum)
    send[...] = jnp.where(upper, a_sum, b_sum).astype(bf16)


def third_sum_kernel(pos, keep, got, *outs):
    for k in range(4):
        block = (pos[5] % ZH) ^ k
        outs[k][...] = (keep[block] + got[block].astype(f32)).astype(outs[k].dtype)


def line_kernel(pos, *refs):
    for k in range(4):
        refs[4][(pos[5] % ZH) ^ k] = refs[k][...]


def row_moment_of(moment, squares):
    mean = jnp.sum(squares, axis=1, keepdims=True) * (1.0 / squares.shape[1])
    return decay_rate * moment + (1.0 - decay_rate) * (mean + tiny_square)


def stats_kernel(pos, near_half, far_half, packed, stats, scaled):
    hidden = near_half.shape[-1]
    upper = pos[5] >= ZH
    cols = jnp.zeros((GR, hidden), f32)
    scaled_cols = jnp.zeros((GR, hidden), f32)
    weights = jnp.zeros((GR, hidden), f32)
    row_total = jnp.zeros((GR, 1), f32)
    for z in range(ZN):
        near, far = near_half[z % ZH].astype(f32), far_half[z % ZH].astype(f32)
        g = jnp.where(upper, far, near) if z < ZH else jnp.where(upper, near, far)
        squares = g * g
        rows = row_moment_of(packed[z, :, hidden : hidden + 1], squares)
        u = g * lax.rsqrt(rows)
        scaled[z] = u
        w = packed[z, :, :hidden]
        cols, scaled_cols, weights = cols + squares, scaled_cols + u * u, weights + w * w
        row_total = row_total + rows
    lane = lax.broadcasted_iota(jnp.int32, (1, hidden), 1)
    total = lambda v: jnp.sum(v, axis=0, keepdims=True)
    scalars = jnp.where(lane == 0, total(row_total), 0.0) + jnp.where(
        lane == 1, jnp.sum(total(weights), axis=1, keepdims=True), 0.0
    )
    stats[...] = jnp.zeros_like(stats)
    stats[0:1], stats[1:2], stats[2:3] = total(cols), total(scaled_cols), scalars


def rows_kernel(width, stats, col_moment, packed, scaled, a_half, b_half, cols_new, inv_cols):
    hidden = scaled.shape[-1]
    lane = lax.broadcasted_iota(jnp.int32, (1, hidden), 1)
    pick = lambda k: jnp.sum(jnp.where(lane == k, stats[2:3], 0.0), axis=1, keepdims=True)
    cols = decay_rate * col_moment[...] + (1.0 - decay_rate) * (
        stats[0:1] * (1.0 / width) + tiny_square
    )
    mean_row = pick(0) * (1.0 / width)
    update_total = mean_row * jnp.sum(stats[1:2] / cols, axis=1, keepdims=True)
    update_rms = jnp.sqrt(update_total * (1.0 / (width * hidden)))
    weight_rms = jnp.sqrt(pick(1) * (1.0 / (width * hidden)))
    factor = (
        jnp.sqrt(mean_row)
        * jnp.maximum(weight_floor, weight_rms)
        / jnp.maximum(1.0, update_rms / clip_level)
    )
    inv = factor * lax.rsqrt(cols)
    cols_new[...], inv_cols[...] = cols, inv
    for z in range(ZN):
        new = packed[z, :, :hidden] - learn_rate * (scaled[z] * inv)
        (a_half, b_half)[z // ZH][z % ZH] = new.astype(bf16)


def return_kernel(pos, near, far, weight, moment, inv_cols, new_weight, delta, rows_new):
    for k, source in enumerate((near, far)):
        rows = pl.ds(pl.multiple_of(GR * (k ^ pos[4]), GR), GR)
        g = source[...]
        moments = row_moment_of(moment[rows], g * g)
        change = g * lax.rsqrt(moments) * inv_cols[...]
        rows_new[rows] = moments
        delta[rows] = change
        new_weight[rows] = weight[rows] - learn_rate * change


def xor_perm(n, k):
    return [(d, d ^ k) for d in range(n)]


def exchange(pieces, axes):
    return [lax.ppermute(pieces[k], axes, xor_perm(4, k)) for k in (1, 2, 3)]


def four_sum(own, got):
    return (own + got[1]) + (got[0] + got[2])


def on_device(tokens, cotangent, weight, row_moment, col_moment):
    tok_rows, width = tokens.shape
    hidden = cotangent.shape[1]
    seg = width // 16
    cuts, y1, y0, xlo, z, core = [lax.axis_index(a) for a in AXES]
    pos = jnp.stack([core, y1, y0, xlo, cuts, reverse_bits(z)]).astype(jnp.int32)
    params = pltpu.CompilerParams(vmem_limit_bytes=12 * 2**20)
    small = pltpu.CompilerParams(vmem_limit_bytes=6 * 2**20)
    cost = pl.CostEstimate(
        flops=64 * tok_rows * seg * hidden, bytes_accessed=16 * 2**20, transcendentals=0
    )
    piece = (2, 2, ZH, GR, hidden)
    whole = pl.BlockSpec((tok_rows, hidden), lambda g, pos: (0, 0))
    piece_spec = pl.BlockSpec((1,) + piece[1:], lambda g, pos: (g, 0, 0, 0, 0))

    def tok_specs(part, step):
        index = cols_at(part, step)
        return [
            pl.BlockSpec((tok_rows, seg), lambda g, pos: (0, pos[0] * 8 + index(g, pos))),
            pl.BlockSpec((tok_rows, seg), lambda g, pos: (0, g)),
        ]

    order = [(0, 0), (1, 0), (0, 1), (1, 1)]
    cotangent2 = lax.ppermute(cotangent, "core", SWAP)
    tokens2 = {}
    for part, step in order:
        index = cols_at(part, step)
        away_cols = pl.pallas_call(
            copy_kernel,
            out_shape=jax.ShapeDtypeStruct((tok_rows, 2 * seg), tokens.dtype),
            grid_spec=pltpu.PrefetchScalarGridSpec(
                num_scalar_prefetch=1,
                grid=(2,),
                in_specs=[
                    pl.BlockSpec(
                        (tok_rows, seg),
                        lambda g, pos, index=index: (0, (1 - pos[0]) * 8 + index(g, pos)),
                    )
                ],
                out_specs=pl.BlockSpec((tok_rows, seg), lambda g, pos: (0, g)),
            ),
            compiler_params=small,
        )(pos, tokens)
        tokens2[part, step] = lax.ppermute(away_cols, "core", SWAP)

    my_weight = lax.dynamic_slice_in_dim(weight, cuts * 32, 32, axis=0)
    my_moment = lax.dynamic_slice_in_dim(row_moment, cuts * 32, 32, axis=0)
    packed = jnp.concatenate(
        [my_weight, jnp.broadcast_to(my_moment[:, None], (32, 128))], axis=1
    )
    packed = lax.ppermute(packed, TURNED, TURN)
    tokens2, cotangent2 = lax.optimization_barrier((tokens2, cotangent2))

    parts, chain = {}, pos
    for part, step in order:
        kept = jax.ShapeDtypeStruct(piece, bf16 if step else f32)
        parts[part, step], parts[part, 2 + step] = pl.pallas_call(
            functools.partial(grad_kernel, part),
            out_shape=[kept, jax.ShapeDtypeStruct(piece, bf16)],
            grid_spec=pltpu.PrefetchScalarGridSpec(
                num_scalar_prefetch=1,
                grid=(2,),
                in_specs=tok_specs(part, step) + [whole] * 2,
                out_specs=[piece_spec] * 2,
            ),
            compiler_params=params,
            cost_estimate=cost,
        )(chain, tokens, tokens2[part, step], cotangent, cotangent2)
        chain, _ = lax.optimization_barrier((pos, parts[part, 2 + step]))
    a_parts, b_parts = [[parts[p, k] for k in range(4)] for p in range(2)]
    a_got, b_got = exchange(a_parts, Y), exchange(b_parts, X)
    a_got, packed = lax.optimization_barrier((a_got, packed))
    packed = lax.psum(
        lax.dynamic_update_slice_in_dim(
            jnp.zeros((ZN,) + packed.shape, f32), packed[None], pos[5], axis=0
        ),
        "z",
    )
    a_sum = a_parts[0] + sum(p.astype(f32) for p in a_got)
    b_sum = b_parts[0] + sum(p.astype(f32) for p in b_got)

    a_parts = [a_sum[k % 2, k // 2] for k in range(4)]
    b_parts = [b_sum[k % 2, k // 2] for k in range(4)]
    a_got = exchange([p.astype(bf16) for p in a_parts], X)
    b_got = exchange([p.astype(bf16) for p in b_parts], Y)
    line, part_line, block = (ZN, GR, hidden), (ZH, GR, hidden), (GR, hidden)
    in_specs = lambda n: [pl.BlockSpec(memory_space=pltpu.SMEM)] + [
        pl.BlockSpec(memory_space=pltpu.VMEM)
    ] * n
    keep, send = pl.pallas_call(
        second_sum_kernel,
        out_shape=[jax.ShapeDtypeStruct(part_line, f32), jax.ShapeDtypeStruct(part_line, bf16)],
        in_specs=in_specs(8),
        compiler_params=small,
    )(pos, a_parts[0], *a_got, b_parts[0], *b_got)

    got = lax.ppermute(send, "z", xor_perm(ZN, 1))
    blocks = pl.pallas_call(
        third_sum_kernel,
        out_shape=[jax.ShapeDtypeStruct(block, f32)] + [jax.ShapeDtypeStruct(block, bf16)] * 3,
        in_specs=in_specs(2),
        compiler_params=small,
    )(pos, keep, got)
    got = [lax.ppermute(blocks[k], "z", xor_perm(ZN, LINE_STEP[k])) for k in (1, 2, 3)]
    g32 = blocks[0] + sum(p.astype(f32) for p in got)

    near = lax.ppermute(g32, TURNED, TURN)
    far = lax.ppermute(g32, ("cuts",) + TURNED, FAR_TURN)

    g16 = g32.astype(bf16)
    got = [lax.ppermute(g16, "z", xor_perm(ZN, LINE_STEP[k])) for k in (1, 2, 3)]
    near_half = pl.pallas_call(
        line_kernel,
        out_shape=jax.ShapeDtypeStruct(part_line, bf16),
        in_specs=in_specs(4),
        compiler_params=small,
    )(pos, g16, *got)
    far_half = lax.ppermute(near_half, "z", xor_perm(ZN, 1))
    far_half, near, far, packed = lax.optimization_barrier((far_half, near, far, packed))

    stats, scaled = pl.pallas_call(
        stats_kernel,
        out_shape=[jax.ShapeDtypeStruct((8, hidden), f32), jax.ShapeDtypeStruct(line, f32)],
        in_specs=in_specs(3),
        compiler_params=small,
    )(pos, near_half, far_half, packed)
    stats = stats + lax.ppermute(stats, "core", SWAP)
    stats = four_sum(stats, exchange([stats] * 4, Y))
    stats = four_sum(stats, exchange([stats] * 4, X))

    row_vector = jax.ShapeDtypeStruct((1, hidden), f32)
    a_half, b_half, cols_new, inv_cols = pl.pallas_call(
        functools.partial(rows_kernel, width),
        out_shape=[jax.ShapeDtypeStruct((ZH, GR, hidden), bf16)] * 2 + [row_vector] * 2,
        compiler_params=small,
    )(stats, col_moment.reshape(1, hidden), packed, scaled)
    a_all = [a_half] + exchange([a_half] * 4, X)
    b_all = [b_half] + exchange([b_half] * 4, Y)
    a_half = jnp.stack([a_all[0], a_all[2], a_all[1], a_all[3]]).reshape(piece)
    b_half = jnp.stack([b_all[0], b_all[2], b_all[1], b_all[3]]).reshape(piece)
    a_half, b_half = lax.optimization_barrier((a_half, b_half))
    a_all, b_all = [a_half], [b_half]
    got = {}
    for k in (2, 1, 3):
        got[0, k] = lax.ppermute(a_half, Y, xor_perm(4, k))
        got[1, k] = lax.ppermute(b_half, X, xor_perm(4, k))
    a_all += [got[0, k] for k in (1, 2, 3)]
    b_all += [got[1, k] for k in (1, 2, 3)]

    slab = jax.ShapeDtypeStruct(weight.shape, f32)
    new_weight, delta, rows_new = pl.pallas_call(
        return_kernel,
        out_shape=[slab, slab, jax.ShapeDtypeStruct((weight.shape[0], 1), f32)],
        in_specs=in_specs(5),
        compiler_params=small,
    )(pos, near, far, weight, row_moment[:, None], inv_cols)
    a_all[2], _ = lax.optimization_barrier((a_all[2], rows_new))

    result = jax.ShapeDtypeStruct((tok_rows, hidden), f32)
    sums = []
    for part, step in [(0, 0), (1, 0), (0, 1), (1, 1)]:
        halves = (a_all, b_all)[part]
        sums = pl.pallas_call(
            functools.partial(apply_kernel, part),
            out_shape=[result, result],
            grid_spec=pltpu.PrefetchScalarGridSpec(
                num_scalar_prefetch=1,
                grid=(2,),
                in_specs=tok_specs(part, step)
                + [piece_spec] * 2
                + [whole] * len(sums),
                out_specs=[whole] * 2,
                scratch_shapes=[pltpu.VMEM((ZH, 2, 2, GR, hidden), bf16)],
            ),
            compiler_params=params,
            cost_estimate=cost,
        )(pos, tokens, tokens2[part, step], halves[step], halves[2 + step], *sums)
    own, away = sums
    summed = own + lax.ppermute(away, "core", SWAP)
    preact = (summed * (1.0 / math.sqrt(width))).astype(bf16)
    return (new_weight, delta, rows_new[:, 0], cols_new[0], preact)


def solution(mesh):
    fine = Mesh(mesh.devices.reshape(SIZES), AXES)
    fsdp = ("y1", "y0", "xlo", "z", "core")
    rows = P(("cuts",) + fsdp, None)
    return jax.shard_map(
        on_device,
        mesh=fine,
        in_specs=(rows, rows, P(fsdp, None), P(fsdp), P()),
        out_specs=(P(fsdp, None), P(fsdp, None), P(fsdp), P(), rows),
        check_vma=False,
    )
```

```python
import functools
import math

import jax
import jax.numpy as jnp
from jax import lax
from jax.experimental import pallas as pl
from jax.experimental.pallas import tpu as pltpu
from jax.sharding import Mesh, PartitionSpec as P

decay_rate = 0.9
tiny_square = 1e-30
clip_level = 1.0
weight_floor = 0.001
learn_rate = 0.1

f32 = jnp.float32
bf16 = jnp.bfloat16

AXES = ("cuts", "y1", "y0", "xlo", "z", "core")
SIZES = (2, 2, 2, 2, 8, 2)
Y = ("y1", "y0")
X = ("cuts", "xlo")
ZN = 8
ZH = 4
GR = 32
SWAP = [(0, 1), (1, 0)]


def reverse_bits(z):
    return (z & 1) * 4 + (z & 2) + (z // 4)


TURN = [
    ((y * ZN + z) * 2 + c, (c * ZN + reverse_bits(z)) * 2 + y)
    for y in range(2)
    for z in range(ZN)
    for c in range(2)
]
FAR_TURN = [(d + 32 * q, e + 32 * (1 - q)) for q in range(2) for d, e in TURN]
TURNED = ("y1", "z", "core")
LINE_STEP = {1: 4, 2: 2, 3: 6}


def cols_at(part, step):
    def index(g, pos):
        row_bit, x_bit = (step, g) if part == 0 else (g, step)
        return (pos[2] ^ row_bit) * 4 + (pos[3] ^ x_bit) * 2 + part

    return index


def chosen(pos, part):
    return (pos[1], pos[4]) if part == 0 else (pos[4], pos[1])


def copy_kernel(pos, src, dst):
    dst[...] = src[...]


def grad_kernel(part, pos, tok, tok2, cot, cot2, out0, out1):
    pick, inner = chosen(pos, part)
    dims = (((0,), (0,)), ((), ()))
    g = lax.dot_general(tok[...], cot[...], dims, preferred_element_type=f32)
    g = g + lax.dot_general(tok2[...], cot2[...], dims, preferred_element_type=f32)
    g = g.reshape(ZH, 2, 2, GR, g.shape[-1])
    for k in range(2):
        first, second = (g[:, 0, k], g[:, 1, k]) if part == 0 else (g[:, k, 0], g[:, k, 1])
        out0[0, k ^ inner] = jnp.where(pick == 0, first, second).astype(out0.dtype)
        out1[0, k ^ inner] = jnp.where(pick == 0, second, first).astype(out1.dtype)


def apply_kernel(part, pos, tok, tok2, piece0, piece1, *refs):
    sums, (own, away, half) = refs[:-3], refs[-3:]
    pick, inner = chosen(pos, part)
    for k in range(2):
        zero, one = piece0[0, k ^ inner], piece1[0, k ^ inner]
        first, second = jnp.where(pick == 0, zero, one), jnp.where(pick == 0, one, zero)
        if part == 0:
            half[:, 0, k], half[:, 1, k] = first, second
        else:
            half[:, k, 0], half[:, k, 1] = first, second
    h = half[...].reshape(-1, half.shape[-1])

    @pl.when(pl.program_id(0) == 0)
    def _():
        for out, begin in zip((own, away), sums or (None, None)):
            out[...] = jnp.zeros_like(out) if begin is None else begin[...]

    own[...] += jnp.dot(tok[...], h, preferred_element_type=f32)
    away[...] += jnp.dot(tok2[...], h, preferred_element_type=f32)


def second_sum_kernel(pos, *refs):
    ins, (keep, send) = refs[:8], refs[8:]
    a_sum, b_sum = [
        ins[n][...] + sum(ins[n + k][...].astype(f32) for k in (1, 2, 3)) for n in (0, 4)
    ]
    upper = pos[5] >= ZH
    keep[...] = jnp.where(upper, b_sum, a_sum)
    send[...] = jnp.where(upper, a_sum, b_sum).astype(bf16)


def third_sum_kernel(pos, keep, got, *outs):
    for k in range(4):
        block = (pos[5] % ZH) ^ k
        outs[k][...] = (keep[block] + got[block].astype(f32)).astype(outs[k].dtype)


def line_kernel(pos, *refs):
    for k in range(4):
        refs[4][(pos[5] % ZH) ^ k] = refs[k][...]


def row_moment_of(moment, squares):
    mean = jnp.sum(squares, axis=1, keepdims=True) * (1.0 / squares.shape[1])
    return decay_rate * moment + (1.0 - decay_rate) * (mean + tiny_square)


def stats_kernel(pos, near_half, far_half, packed, stats, scaled):
    hidden = near_half.shape[-1]
    upper = pos[5] >= ZH
    cols = jnp.zeros((GR, hidden), f32)
    scaled_cols = jnp.zeros((GR, hidden), f32)
    weights = jnp.zeros((GR, hidden), f32)
    row_total = jnp.zeros((GR, 1), f32)
    for z in range(ZN):
        near, far = near_half[z % ZH].astype(f32), far_half[z % ZH].astype(f32)
        g = jnp.where(upper, far, near) if z < ZH else jnp.where(upper, near, far)
        squares = g * g
        rows = row_moment_of(packed[reverse_bits(z), :, hidden : hidden + 1], squares)
        u = g * lax.rsqrt(rows)
        scaled[z] = u
        w = packed[reverse_bits(z), :, :hidden]
        cols, scaled_cols, weights = cols + squares, scaled_cols + u * u, weights + w * w
        row_total = row_total + rows
    lane = lax.broadcasted_iota(jnp.int32, (1, hidden), 1)
    total = lambda v: jnp.sum(v, axis=0, keepdims=True)
    scalars = jnp.where(lane == 0, total(row_total), 0.0) + jnp.where(
        lane == 1, jnp.sum(total(weights), axis=1, keepdims=True), 0.0
    )
    stats[...] = jnp.zeros_like(stats)
    stats[0:1], stats[1:2], stats[2:3] = total(cols), total(scaled_cols), scalars


def rows_kernel(width, stats, col_moment, packed, scaled, a_half, b_half, cols_new, inv_cols):
    hidden = scaled.shape[-1]
    lane = lax.broadcasted_iota(jnp.int32, (1, hidden), 1)
    pick = lambda k: jnp.sum(jnp.where(lane == k, stats[2:3], 0.0), axis=1, keepdims=True)
    cols = decay_rate * col_moment[...] + (1.0 - decay_rate) * (
        stats[0:1] * (1.0 / width) + tiny_square
    )
    mean_row = pick(0) * (1.0 / width)
    update_total = mean_row * jnp.sum(stats[1:2] / cols, axis=1, keepdims=True)
    update_rms = jnp.sqrt(update_total * (1.0 / (width * hidden)))
    weight_rms = jnp.sqrt(pick(1) * (1.0 / (width * hidden)))
    factor = (
        jnp.sqrt(mean_row)
        * jnp.maximum(weight_floor, weight_rms)
        / jnp.maximum(1.0, update_rms / clip_level)
    )
    inv = factor * lax.rsqrt(cols)
    cols_new[...], inv_cols[...] = cols, inv
    for z in range(ZN):
        new = packed[reverse_bits(z), :, :hidden] - learn_rate * (scaled[z] * inv)
        (a_half, b_half)[z // ZH][z % ZH] = new.astype(bf16)


def return_kernel(pos, near, far, weight, moment, inv_cols, new_weight, delta, rows_new):
    for k, source in enumerate((near, far)):
        rows = pl.ds(pl.multiple_of(GR * (k ^ pos[4]), GR), GR)
        g = source[...]
        moments = row_moment_of(moment[rows], g * g)
        change = g * lax.rsqrt(moments) * inv_cols[...]
        rows_new[rows] = moments
        delta[rows] = change
        new_weight[rows] = weight[rows] - learn_rate * change


def xor_perm(n, k):
    return [(d, d ^ k) for d in range(n)]


def exchange(pieces, axes):
    return [lax.ppermute(pieces[k], axes, xor_perm(4, k)) for k in (1, 2, 3)]


def four_sum(own, got):
    return (own + got[1]) + (got[0] + got[2])


def on_device(tokens, cotangent, weight, row_moment, col_moment):
    tok_rows, width = tokens.shape
    hidden = cotangent.shape[1]
    seg = width // 16
    cuts, y1, y0, xlo, z, core = [lax.axis_index(a) for a in AXES]
    pos = jnp.stack([core, y1, y0, xlo, cuts, reverse_bits(z)]).astype(jnp.int32)
    params = pltpu.CompilerParams(vmem_limit_bytes=12 * 2**20)
    small = pltpu.CompilerParams(vmem_limit_bytes=6 * 2**20)
    cost = pl.CostEstimate(
        flops=64 * tok_rows * seg * hidden, bytes_accessed=16 * 2**20, transcendentals=0
    )
    piece = (2, 2, ZH, GR, hidden)
    whole = pl.BlockSpec((tok_rows, hidden), lambda g, pos: (0, 0))
    piece_spec = pl.BlockSpec((1,) + piece[1:], lambda g, pos: (g, 0, 0, 0, 0))

    def tok_specs(part, step):
        index = cols_at(part, step)
        return [
            pl.BlockSpec((tok_rows, seg), lambda g, pos: (0, pos[0] * 8 + index(g, pos))),
            pl.BlockSpec((tok_rows, seg), lambda g, pos: (0, g)),
        ]

    order = [(0, 0), (1, 0), (0, 1), (1, 1)]
    cotangent2 = lax.ppermute(cotangent, "core", SWAP)
    tokens2 = {}
    for part, step in order:
        index = cols_at(part, step)
        away_cols = pl.pallas_call(
            copy_kernel,
            out_shape=jax.ShapeDtypeStruct((tok_rows, 2 * seg), tokens.dtype),
            grid_spec=pltpu.PrefetchScalarGridSpec(
                num_scalar_prefetch=1,
                grid=(2,),
                in_specs=[
                    pl.BlockSpec(
                        (tok_rows, seg),
                        lambda g, pos, index=index: (0, (1 - pos[0]) * 8 + index(g, pos)),
                    )
                ],
                out_specs=pl.BlockSpec((tok_rows, seg), lambda g, pos: (0, g)),
            ),
            compiler_params=small,
        )(pos, tokens)
        tokens2[part, step] = lax.ppermute(away_cols, "core", SWAP)

    my_weight = lax.dynamic_slice_in_dim(weight, cuts * 32, 32, axis=0)
    my_moment = lax.dynamic_slice_in_dim(row_moment, cuts * 32, 32, axis=0)
    packed = jnp.concatenate(
        [my_weight, jnp.broadcast_to(my_moment[:, None], (32, 128))], axis=1
    )
    packed = lax.ppermute(packed, TURNED, TURN)
    tokens2, cotangent2 = lax.optimization_barrier((tokens2, cotangent2))

    parts, chain = {}, pos
    for part, step in order:
        kept = jax.ShapeDtypeStruct(piece, bf16 if step else f32)
        parts[part, step], parts[part, 2 + step] = pl.pallas_call(
            functools.partial(grad_kernel, part),
            out_shape=[kept, jax.ShapeDtypeStruct(piece, bf16)],
            grid_spec=pltpu.PrefetchScalarGridSpec(
                num_scalar_prefetch=1,
                grid=(2,),
                in_specs=tok_specs(part, step) + [whole] * 2,
                out_specs=[piece_spec] * 2,
            ),
            compiler_params=params,
            cost_estimate=cost,
        )(chain, tokens, tokens2[part, step], cotangent, cotangent2)
        chain, _ = lax.optimization_barrier((pos, parts[part, 2 + step]))
    a_parts, b_parts = [[parts[p, k] for k in range(4)] for p in range(2)]
    a_got, b_got = exchange(a_parts, Y), exchange(b_parts, X)
    a_got, packed = lax.optimization_barrier((a_got, packed))
    packed = lax.all_to_all(
        jnp.broadcast_to(packed[None], (ZN,) + packed.shape), "z", 0, 0, tiled=True
    )
    a_sum = a_parts[0] + sum(p.astype(f32) for p in a_got)
    b_sum = b_parts[0] + sum(p.astype(f32) for p in b_got)

    a_parts = [a_sum[k % 2, k // 2] for k in range(4)]
    b_parts = [b_sum[k % 2, k // 2] for k in range(4)]
    a_got = exchange([p.astype(bf16) for p in a_parts], X)
    b_got = exchange([p.astype(bf16) for p in b_parts], Y)
    b_got, packed = lax.optimization_barrier((b_got, packed))
    line, part_line, block = (ZN, GR, hidden), (ZH, GR, hidden), (GR, hidden)
    in_specs = lambda n: [pl.BlockSpec(memory_space=pltpu.SMEM)] + [
        pl.BlockSpec(memory_space=pltpu.VMEM)
    ] * n
    keep, send = pl.pallas_call(
        second_sum_kernel,
        out_shape=[jax.ShapeDtypeStruct(part_line, f32), jax.ShapeDtypeStruct(part_line, bf16)],
        in_specs=in_specs(8),
        compiler_params=small,
    )(pos, a_parts[0], *a_got, b_parts[0], *b_got)

    got = lax.ppermute(send, "z", xor_perm(ZN, 1))
    blocks = pl.pallas_call(
        third_sum_kernel,
        out_shape=[jax.ShapeDtypeStruct(block, f32)] + [jax.ShapeDtypeStruct(block, bf16)] * 3,
        in_specs=in_specs(2),
        compiler_params=small,
    )(pos, keep, got)
    got = [lax.ppermute(blocks[k], "z", xor_perm(ZN, LINE_STEP[k])) for k in (1, 2, 3)]
    g32 = blocks[0] + sum(p.astype(f32) for p in got)

    near = lax.ppermute(g32, TURNED, TURN)
    far = lax.ppermute(g32, ("cuts",) + TURNED, FAR_TURN)

    g16 = g32.astype(bf16)
    got = [lax.ppermute(g16, "z", xor_perm(ZN, LINE_STEP[k])) for k in (1, 2, 3)]
    near_half = pl.pallas_call(
        line_kernel,
        out_shape=jax.ShapeDtypeStruct(part_line, bf16),
        in_specs=in_specs(4),
        compiler_params=small,
    )(pos, g16, *got)
    far_half = lax.ppermute(near_half, "z", xor_perm(ZN, 1))
    far_half, near, far = lax.optimization_barrier((far_half, near, far))

    stats, scaled = pl.pallas_call(
        stats_kernel,
        out_shape=[jax.ShapeDtypeStruct((8, hidden), f32), jax.ShapeDtypeStruct(line, f32)],
        in_specs=in_specs(3),
        compiler_params=small,
    )(pos, near_half, far_half, packed)
    stats = stats + lax.ppermute(stats, "core", SWAP)
    stats = four_sum(stats, exchange([stats] * 4, Y))
    stats = four_sum(stats, exchange([stats] * 4, X))

    row_vector = jax.ShapeDtypeStruct((1, hidden), f32)
    a_half, b_half, cols_new, inv_cols = pl.pallas_call(
        functools.partial(rows_kernel, width),
        out_shape=[jax.ShapeDtypeStruct((ZH, GR, hidden), bf16)] * 2 + [row_vector] * 2,
        compiler_params=small,
    )(stats, col_moment.reshape(1, hidden), packed, scaled)
    a_all = [a_half] + exchange([a_half] * 4, X)
    b_all = [b_half] + exchange([b_half] * 4, Y)
    a_half = jnp.stack([a_all[0], a_all[2], a_all[1], a_all[3]]).reshape(piece)
    b_half = jnp.stack([b_all[0], b_all[2], b_all[1], b_all[3]]).reshape(piece)
    a_half, b_half = lax.optimization_barrier((a_half, b_half))
    a_all, b_all = [a_half], [b_half]
    got = {}
    for k in (2, 1, 3):
        got[0, k] = lax.ppermute(a_half, Y, xor_perm(4, k))
        got[1, k] = lax.ppermute(b_half, X, xor_perm(4, k))
    a_all += [got[0, k] for k in (1, 2, 3)]
    b_all += [got[1, k] for k in (1, 2, 3)]

    slab = jax.ShapeDtypeStruct(weight.shape, f32)
    new_weight, delta, rows_new = pl.pallas_call(
        return_kernel,
        out_shape=[slab, slab, jax.ShapeDtypeStruct((weight.shape[0], 1), f32)],
        in_specs=in_specs(5),
        compiler_params=small,
    )(pos, near, far, weight, row_moment[:, None], inv_cols)
    a_all[2], _ = lax.optimization_barrier((a_all[2], rows_new))

    result = jax.ShapeDtypeStruct((tok_rows, hidden), f32)
    sums = []
    for part, step in [(0, 0), (1, 0), (0, 1), (1, 1)]:
        halves = (a_all, b_all)[part]
        sums = pl.pallas_call(
            functools.partial(apply_kernel, part),
            out_shape=[result, result],
            grid_spec=pltpu.PrefetchScalarGridSpec(
                num_scalar_prefetch=1,
                grid=(2,),
                in_specs=tok_specs(part, step)
                + [piece_spec] * 2
                + [whole] * len(sums),
                out_specs=[whole] * 2,
                scratch_shapes=[pltpu.VMEM((ZH, 2, 2, GR, hidden), bf16)],
            ),
            compiler_params=params,
            cost_estimate=cost,
        )(pos, tokens, tokens2[part, step], halves[step], halves[2 + step], *sums)
    own, away = sums
    summed = own + lax.ppermute(away, "core", SWAP)
    preact = (summed * (1.0 / math.sqrt(width))).astype(bf16)
    return (new_weight, delta, rows_new[:, 0], cols_new[0], preact)


def solution(mesh):
    fine = Mesh(mesh.devices.reshape(SIZES), AXES)
    fsdp = ("y1", "y0", "xlo", "z", "core")
    rows = P(("cuts",) + fsdp, None)
    return jax.shard_map(
        on_device,
        mesh=fine,
        in_specs=(rows, rows, P(fsdp, None), P(fsdp), P()),
        out_specs=(P(fsdp, None), P(fsdp, None), P(fsdp), P(), rows),
        check_vma=False,
    )
```

```python
import functools
import math

import jax
import jax.numpy as jnp
from jax import lax
from jax.experimental import pallas as pl
from jax.experimental.pallas import tpu as pltpu
from jax.sharding import Mesh, PartitionSpec as P

decay_rate = 0.9
tiny_square = 1e-30
clip_level = 1.0
weight_floor = 0.001
learn_rate = 0.1

f32 = jnp.float32
bf16 = jnp.bfloat16

AXES = ("cuts", "y1", "y0", "xlo", "z", "core")
SIZES = (2, 2, 2, 2, 8, 2)
Y = ("y1", "y0")
X = ("cuts", "xlo")
ZN = 8
ZH = 4
GR = 32
SWAP = [(0, 1), (1, 0)]


def reverse_bits(z):
    return (z & 1) * 4 + (z & 2) + (z // 4)


TURN = [
    ((y * ZN + z) * 2 + c, (c * ZN + reverse_bits(z)) * 2 + y)
    for y in range(2)
    for z in range(ZN)
    for c in range(2)
]
FAR_TURN = [(d + 32 * q, e + 32 * (1 - q)) for q in range(2) for d, e in TURN]
TURNED = ("y1", "z", "core")
LINE_STEP = {1: 4, 2: 2, 3: 6}


def cols_at(part, step):
    def index(g, pos):
        row_bit, x_bit = (step, g) if part == 0 else (g, step)
        return (pos[2] ^ row_bit) * 4 + (pos[3] ^ x_bit) * 2 + part

    return index


def chosen(pos, part):
    return (pos[1], pos[4]) if part == 0 else (pos[4], pos[1])


def copy_kernel(pos, src, dst):
    dst[...] = src[...]


def grad_kernel(part, pos, tok, tok2, cot, cot2, out0, out1):
    pick, inner = chosen(pos, part)
    dims = (((0,), (0,)), ((), ()))
    g = lax.dot_general(tok[...], cot[...], dims, preferred_element_type=f32)
    g = g + lax.dot_general(tok2[...], cot2[...], dims, preferred_element_type=f32)
    g = g.reshape(ZH, 2, 2, GR, g.shape[-1])
    for k in range(2):
        first, second = (g[:, 0, k], g[:, 1, k]) if part == 0 else (g[:, k, 0], g[:, k, 1])
        out0[0, k ^ inner] = jnp.where(pick == 0, first, second).astype(out0.dtype)
        out1[0, k ^ inner] = jnp.where(pick == 0, second, first).astype(out1.dtype)


def apply_kernel(part, pos, tok, tok2, piece0, piece1, *refs):
    sums, (own, away, half) = refs[:-3], refs[-3:]
    pick, inner = chosen(pos, part)
    for k in range(2):
        zero, one = piece0[0, k ^ inner], piece1[0, k ^ inner]
        first, second = jnp.where(pick == 0, zero, one), jnp.where(pick == 0, one, zero)
        if part == 0:
            half[:, 0, k], half[:, 1, k] = first, second
        else:
            half[:, k, 0], half[:, k, 1] = first, second
    h = half[...].reshape(-1, half.shape[-1])

    @pl.when(pl.program_id(0) == 0)
    def _():
        for out, begin in zip((own, away), sums or (None, None)):
            out[...] = jnp.zeros_like(out) if begin is None else begin[...]

    own[...] += jnp.dot(tok[...], h, preferred_element_type=f32)
    away[...] += jnp.dot(tok2[...], h, preferred_element_type=f32)


def second_sum_kernel(pos, *refs):
    ins, (keep, send) = refs[:8], refs[8:]
    a_sum, b_sum = [
        ins[n][...] + sum(ins[n + k][...].astype(f32) for k in (1, 2, 3)) for n in (0, 4)
    ]
    upper = pos[5] >= ZH
    keep[...] = jnp.where(upper, b_sum, a_sum)
    send[...] = jnp.where(upper, a_sum, b_sum).astype(bf16)


def third_sum_kernel(pos, keep, got, *outs):
    for k in range(4):
        block = (pos[5] % ZH) ^ k
        outs[k][...] = (keep[block] + got[block].astype(f32)).astype(outs[k].dtype)


def line_kernel(pos, *refs):
    for k in range(4):
        refs[4][(pos[5] % ZH) ^ k] = refs[k][...]


def row_moment_of(moment, squares):
    mean = jnp.sum(squares, axis=1, keepdims=True) * (1.0 / squares.shape[1])
    return decay_rate * moment + (1.0 - decay_rate) * (mean + tiny_square)


def stats_kernel(g32, packed, stats, block):
    hidden = g32.shape[-1]
    g, w = g32[...], packed[:, :hidden]
    squares = g * g
    rows = row_moment_of(packed[:, hidden : hidden + 1], squares)
    u = g * lax.rsqrt(rows)
    block[:, :hidden], block[:, hidden:] = w, u
    lane = lax.broadcasted_iota(jnp.int32, (1, hidden), 1)
    total = lambda v: jnp.sum(v, axis=0, keepdims=True)
    scalars = jnp.where(lane == 0, total(rows), 0.0) + jnp.where(
        lane == 1, jnp.sum(total(w * w), axis=1, keepdims=True), 0.0
    )
    stats[...] = jnp.zeros_like(stats)
    stats[0:1], stats[1:2], stats[2:3] = total(squares), total(u * u), scalars


def rows_kernel(width, pos, stats, col_moment, near_half, far_half, *outs):
    a_half, b_half, cols_new, inv_cols = outs
    hidden = stats.shape[-1]
    upper = pos[5] >= ZH
    lane = lax.broadcasted_iota(jnp.int32, (1, hidden), 1)
    pick = lambda k: jnp.sum(jnp.where(lane == k, stats[2:3], 0.0), axis=1, keepdims=True)
    cols = decay_rate * col_moment[...] + (1.0 - decay_rate) * (
        stats[0:1] * (1.0 / width) + tiny_square
    )
    mean_row = pick(0) * (1.0 / width)
    update_total = mean_row * jnp.sum(stats[1:2] / cols, axis=1, keepdims=True)
    update_rms = jnp.sqrt(update_total * (1.0 / (width * hidden)))
    weight_rms = jnp.sqrt(pick(1) * (1.0 / (width * hidden)))
    factor = (
        jnp.sqrt(mean_row)
        * jnp.maximum(weight_floor, weight_rms)
        / jnp.maximum(1.0, update_rms / clip_level)
    )
    inv = factor * lax.rsqrt(cols)
    cols_new[...], inv_cols[...] = cols, inv
    for z in range(ZH):
        near, far = [
            (v[z, :, :hidden] - learn_rate * (v[z, :, hidden:] * inv)).astype(bf16)
            for v in (near_half, far_half)
        ]
        a_half[z] = jnp.where(upper, far, near)
        b_half[z] = jnp.where(upper, near, far)


def return_kernel(pos, near, far, weight, moment, inv_cols, new_weight, delta, rows_new):
    for k, source in enumerate((near, far)):
        rows = pl.ds(pl.multiple_of(GR * (k ^ pos[4]), GR), GR)
        g = source[...]
        moments = row_moment_of(moment[rows], g * g)
        change = g * lax.rsqrt(moments) * inv_cols[...]
        rows_new[rows] = moments
        delta[rows] = change
        new_weight[rows] = weight[rows] - learn_rate * change


def xor_perm(n, k):
    return [(d, d ^ k) for d in range(n)]


def exchange(pieces, axes):
    return [lax.ppermute(pieces[k], axes, xor_perm(4, k)) for k in (1, 2, 3)]


def four_sum(own, got):
    return (own + got[1]) + (got[0] + got[2])


def on_device(tokens, cotangent, weight, row_moment, col_moment):
    tok_rows, width = tokens.shape
    hidden = cotangent.shape[1]
    seg = width // 16
    cuts, y1, y0, xlo, z, core = [lax.axis_index(a) for a in AXES]
    pos = jnp.stack([core, y1, y0, xlo, cuts, reverse_bits(z)]).astype(jnp.int32)
    params = pltpu.CompilerParams(vmem_limit_bytes=16 * 2**20)
    small = pltpu.CompilerParams(vmem_limit_bytes=6 * 2**20)
    cost = pl.CostEstimate(
        flops=64 * tok_rows * seg * hidden, bytes_accessed=16 * 2**20, transcendentals=0
    )
    piece = (2, 2, ZH, GR, hidden)
    whole = pl.BlockSpec((tok_rows, hidden), lambda g, pos: (0, 0))
    piece_spec = pl.BlockSpec((1,) + piece[1:], lambda g, pos: (g, 0, 0, 0, 0))

    def tok_specs(part, step):
        index = cols_at(part, step)
        return [
            pl.BlockSpec((tok_rows, seg), lambda g, pos: (0, pos[0] * 8 + index(g, pos))),
            pl.BlockSpec((tok_rows, seg), lambda g, pos: (0, g)),
        ]

    order = [(0, 1), (1, 1), (0, 0), (1, 0)]
    cotangent2 = lax.ppermute(cotangent, "core", SWAP)
    tokens2 = {}
    for part, step in order:
        index = cols_at(part, step)
        away_cols = pl.pallas_call(
            copy_kernel,
            out_shape=jax.ShapeDtypeStruct((tok_rows, 2 * seg), tokens.dtype),
            grid_spec=pltpu.PrefetchScalarGridSpec(
                num_scalar_prefetch=1,
                grid=(2,),
                in_specs=[
                    pl.BlockSpec(
                        (tok_rows, seg),
                        lambda g, pos, index=index: (0, (1 - pos[0]) * 8 + index(g, pos)),
                    )
                ],
                out_specs=pl.BlockSpec((tok_rows, seg), lambda g, pos: (0, g)),
            ),
            compiler_params=small,
        )(pos, tokens)
        tokens2[part, step] = lax.ppermute(away_cols, "core", SWAP)

    my_weight = lax.dynamic_slice_in_dim(weight, cuts * 32, 32, axis=0)
    my_moment = lax.dynamic_slice_in_dim(row_moment, cuts * 32, 32, axis=0)
    packed = jnp.concatenate(
        [my_weight, jnp.broadcast_to(my_moment[:, None], (32, 128))], axis=1
    )
    packed = lax.ppermute(packed, TURNED, TURN)

    parts = {}
    for part, step in order:
        kept = jax.ShapeDtypeStruct(piece, bf16 if step else f32)
        parts[part, step], parts[part, 2 + step] = pl.pallas_call(
            functools.partial(grad_kernel, part),
            out_shape=[kept, jax.ShapeDtypeStruct(piece, bf16)],
            grid_spec=pltpu.PrefetchScalarGridSpec(
                num_scalar_prefetch=1,
                grid=(2,),
                in_specs=tok_specs(part, step) + [whole] * 2,
                out_specs=[piece_spec] * 2,
            ),
            compiler_params=params,
            cost_estimate=cost,
        )(pos, tokens, tokens2[part, step], cotangent, cotangent2)
    a_parts, b_parts = [[parts[p, k] for k in range(4)] for p in range(2)]
    a_got, b_got = exchange(a_parts, Y), exchange(b_parts, X)
    a_sum = a_parts[0] + sum(p.astype(f32) for p in a_got)
    b_sum = b_parts[0] + sum(p.astype(f32) for p in b_got)

    a_parts = [a_sum[k % 2, k // 2] for k in range(4)]
    b_parts = [b_sum[k % 2, k // 2] for k in range(4)]
    a_got = exchange([p.astype(bf16) for p in a_parts], X)
    b_got = exchange([p.astype(bf16) for p in b_parts], Y)
    b_got, packed = lax.optimization_barrier((b_got, packed))
    line, part_line, block = (ZN, GR, hidden), (ZH, GR, hidden), (GR, hidden)
    in_specs = lambda n: [pl.BlockSpec(memory_space=pltpu.SMEM)] + [
        pl.BlockSpec(memory_space=pltpu.VMEM)
    ] * n
    keep, send = pl.pallas_call(
        second_sum_kernel,
        out_shape=[jax.ShapeDtypeStruct(part_line, f32), jax.ShapeDtypeStruct(part_line, bf16)],
        in_specs=in_specs(8),
        compiler_params=small,
    )(pos, a_parts[0], *a_got, b_parts[0], *b_got)

    got = lax.ppermute(send, "z", xor_perm(ZN, 1))
    blocks = pl.pallas_call(
        third_sum_kernel,
        out_shape=[jax.ShapeDtypeStruct(block, f32)] + [jax.ShapeDtypeStruct(block, bf16)] * 3,
        in_specs=in_specs(2),
        compiler_params=small,
    )(pos, keep, got)
    got = [lax.ppermute(blocks[k], "z", xor_perm(ZN, LINE_STEP[k])) for k in (1, 2, 3)]
    g32 = blocks[0] + sum(p.astype(f32) for p in got)

    near = lax.ppermute(g32, TURNED, TURN)
    far = lax.ppermute(g32, ("cuts",) + TURNED, FAR_TURN)

    stats, own = pl.pallas_call(
        stats_kernel,
        out_shape=[
            jax.ShapeDtypeStruct((8, hidden), f32),
            jax.ShapeDtypeStruct((GR, 2 * hidden), f32),
        ],
        compiler_params=small,
    )(g32, packed)
    got = [lax.ppermute(own, "z", xor_perm(ZN, LINE_STEP[k])) for k in (1, 2, 3)]
    near_half = pl.pallas_call(
        line_kernel,
        out_shape=jax.ShapeDtypeStruct((ZH,) + own.shape, f32),
        in_specs=in_specs(4),
        compiler_params=small,
    )(pos, own, *got)
    far_half = lax.ppermute(near_half, "z", xor_perm(ZN, 1))
    stats = stats + lax.ppermute(stats, "core", SWAP)
    stats = four_sum(stats, exchange([stats] * 4, Y))
    stats = four_sum(stats, exchange([stats] * 4, X))
    stats = four_sum(stats, [lax.ppermute(stats, "z", xor_perm(ZN, k)) for k in (1, 2, 3)])
    stats = stats + lax.ppermute(stats, "z", xor_perm(ZN, 4))
    stats, near, far = lax.optimization_barrier((stats, near, far))

    row_vector = jax.ShapeDtypeStruct((1, hidden), f32)
    a_half, b_half, cols_new, inv_cols = pl.pallas_call(
        functools.partial(rows_kernel, width),
        out_shape=[jax.ShapeDtypeStruct((ZH, GR, hidden), bf16)] * 2 + [row_vector] * 2,
        in_specs=in_specs(4),
        compiler_params=small,
    )(pos, stats, col_moment.reshape(1, hidden), near_half, far_half)
    a_all = [a_half] + exchange([a_half] * 4, X)
    b_all = [b_half] + exchange([b_half] * 4, Y)
    a_half = jnp.stack([a_all[0], a_all[2], a_all[1], a_all[3]]).reshape(piece)
    b_half = jnp.stack([b_all[0], b_all[2], b_all[1], b_all[3]]).reshape(piece)
    slab = jax.ShapeDtypeStruct(weight.shape, f32)
    new_weight, delta, rows_new = pl.pallas_call(
        return_kernel,
        out_shape=[slab, slab, jax.ShapeDtypeStruct((weight.shape[0], 1), f32)],
        in_specs=in_specs(5),
        compiler_params=small,
    )(pos, near, far, weight, row_moment[:, None], inv_cols)
    a_half, b_half, rows_new = lax.optimization_barrier((a_half, b_half, rows_new))
    a_all, b_all = [a_half], [b_half]
    got = {}
    for k in (2, 1, 3):
        got[0, k] = lax.ppermute(a_half, Y, xor_perm(4, k))
        got[1, k] = lax.ppermute(b_half, X, xor_perm(4, k))
    a_all += [got[0, k] for k in (1, 2, 3)]
    b_all += [got[1, k] for k in (1, 2, 3)]

    result = jax.ShapeDtypeStruct((tok_rows, hidden), f32)
    sums = []
    for part, step in [(0, 0), (1, 0), (0, 1), (1, 1)]:
        halves = (a_all, b_all)[part]
        sums = pl.pallas_call(
            functools.partial(apply_kernel, part),
            out_shape=[result, result],
            grid_spec=pltpu.PrefetchScalarGridSpec(
                num_scalar_prefetch=1,
                grid=(2,),
                in_specs=tok_specs(part, step)
                + [piece_spec] * 2
                + [whole] * len(sums),
                out_specs=[whole] * 2,
                scratch_shapes=[pltpu.VMEM((ZH, 2, 2, GR, hidden), bf16)],
            ),
            compiler_params=params,
            cost_estimate=cost,
        )(pos, tokens, tokens2[part, step], halves[step], halves[2 + step], *sums)
    own, away = sums
    summed = own + lax.ppermute(away, "core", SWAP)
    preact = (summed * (1.0 / math.sqrt(width))).astype(bf16)
    return (new_weight, delta, rows_new[:, 0], cols_new[0], preact)


def solution(mesh):
    fine = Mesh(mesh.devices.reshape(SIZES), AXES)
    fsdp = ("y1", "y0", "xlo", "z", "core")
    rows = P(("cuts",) + fsdp, None)
    return jax.shard_map(
        on_device,
        mesh=fine,
        in_specs=(rows, rows, P(fsdp, None), P(fsdp), P()),
        out_specs=(P(fsdp, None), P(fsdp, None), P(fsdp), P(), rows),
        check_vma=False,
    )
```

```python
import functools
import math

import jax
import jax.numpy as jnp
from jax import lax
from jax.experimental import pallas as pl
from jax.experimental.pallas import tpu as pltpu
from jax.sharding import Mesh, PartitionSpec as P

decay_rate = 0.9
tiny_square = 1e-30
clip_level = 1.0
weight_floor = 0.001
learn_rate = 0.1

f32 = jnp.float32
bf16 = jnp.bfloat16

AXES = ("cuts", "y1", "y0", "xlo", "z", "core")
SIZES = (2, 2, 2, 2, 8, 2)
Y = ("y1", "y0")
X = ("cuts", "xlo")
ZN = 8
ZH = 4
GR = 32
SWAP = [(0, 1), (1, 0)]


def reverse_bits(z):
    return (z & 1) * 4 + (z & 2) + ((z >> 2) & 1)


TURN = [
    ((y * ZN + z) * 2 + c, (c * ZN + reverse_bits(z)) * 2 + y)
    for y in range(2)
    for z in range(ZN)
    for c in range(2)
]
FAR_TURN = [(d + 32 * q, e + 32 * (1 - q)) for q in range(2) for d, e in TURN]
TURNED = ("y1", "z", "core")
LINE_STEP = {1: 4, 2: 2, 3: 6}


def cols_at(part, step):
    def index(g, pos):
        row_bit, x_bit = (step, g) if part == 0 else (g, step)
        return (pos[2] ^ row_bit) * 4 + (pos[3] ^ x_bit) * 2 + part

    return index


def chosen(pos, part):
    return (pos[1], pos[4]) if part == 0 else (pos[4], pos[1])


def pack_kernel(pos, weight, moment, out):
    rows = pl.ds(pl.multiple_of(GR * pos[4], GR), GR)
    hidden = weight.shape[-1]
    out[:, :hidden] = weight[rows]
    out[:, hidden:] = jnp.broadcast_to(moment[rows], (GR, out.shape[-1] - hidden))


def copy_kernel(pos, src, dst):
    dst[...] = src[...]


def grad_kernel(part, pos, tok, tok2, cot, cot2, out0, out1):
    pick, inner = chosen(pos, part)
    dims = (((0,), (0,)), ((), ()))
    g = lax.dot_general(tok[...], cot[...], dims, preferred_element_type=f32)
    g = g + lax.dot_general(tok2[...], cot2[...], dims, preferred_element_type=f32)
    g = g.reshape(ZH, 2, 2, GR, g.shape[-1])
    for k in range(2):
        first, second = (g[:, 0, k], g[:, 1, k]) if part == 0 else (g[:, k, 0], g[:, k, 1])
        out0[0, k ^ inner] = jnp.where(pick == 0, first, second).astype(out0.dtype)
        out1[0, k ^ inner] = jnp.where(pick == 0, second, first).astype(out1.dtype)


def apply_kernel(part, pos, tok, tok2, piece0, piece1, *refs):
    sums, (own, away, half) = refs[:-3], refs[-3:]
    pick, inner = chosen(pos, part)
    for k in range(2):
        zero, one = piece0[0, k ^ inner], piece1[0, k ^ inner]
        first, second = jnp.where(pick == 0, zero, one), jnp.where(pick == 0, one, zero)
        if part == 0:
            half[:, 0, k], half[:, 1, k] = first, second
        else:
            half[:, k, 0], half[:, k, 1] = first, second
    h = half[...].reshape(-1, half.shape[-1])

    @pl.when(pl.program_id(0) == 0)
    def _():
        for out, begin in zip((own, away), sums or (None, None)):
            out[...] = jnp.zeros_like(out) if begin is None else begin[...]

    own[...] += jnp.dot(tok[...], h, preferred_element_type=f32)
    away[...] += jnp.dot(tok2[...], h, preferred_element_type=f32)


def second_sum_kernel(pos, *refs):
    ins, (keep, send) = refs[:8], refs[8:]
    a_sum, b_sum = [
        ins[n][...] + sum(ins[n + k][...].astype(f32) for k in (1, 2, 3)) for n in (0, 4)
    ]
    upper = pos[5] >= ZH
    keep[...] = jnp.where(upper, b_sum, a_sum)
    send[...] = jnp.where(upper, a_sum, b_sum).astype(bf16)


def third_sum_kernel(pos, keep, got, *outs):
    for k in range(4):
        block = (pos[5] % ZH) ^ k
        outs[k][...] = (keep[block] + got[block].astype(f32)).astype(outs[k].dtype)


def line_kernel(pos, *refs):
    for k in range(4):
        refs[4][(pos[5] % ZH) ^ k] = refs[k][...]


def row_moment_of(moment, squares):
    mean = jnp.sum(squares, axis=1, keepdims=True) * (1.0 / squares.shape[1])
    return decay_rate * moment + (1.0 - decay_rate) * (mean + tiny_square)


def stats_kernel(g32, packed, stats, block):
    hidden = g32.shape[-1]
    g, w = g32[...], packed[:, :hidden]
    squares = g * g
    rows = row_moment_of(packed[:, hidden : hidden + 1], squares)
    u = g * lax.rsqrt(rows)
    block[:, :hidden], block[:, hidden:] = w, u
    lane = lax.broadcasted_iota(jnp.int32, (1, hidden), 1)
    total = lambda v: jnp.sum(v, axis=0, keepdims=True)
    scalars = jnp.where(lane == 0, total(rows), 0.0) + jnp.where(
        lane == 1, jnp.sum(total(w * w), axis=1, keepdims=True), 0.0
    )
    stats[...] = jnp.zeros_like(stats)
    stats[0:1], stats[1:2], stats[2:3] = total(squares), total(u * u), scalars


def rows_kernel(width, pos, stats, col_moment, near_half, far_half, *outs):
    a_half, b_half, cols_new, inv_cols = outs
    hidden = stats.shape[-1]
    upper = pos[5] >= ZH
    lane = lax.broadcasted_iota(jnp.int32, (1, hidden), 1)
    pick = lambda k: jnp.sum(jnp.where(lane == k, stats[2:3], 0.0), axis=1, keepdims=True)
    cols = decay_rate * col_moment[...] + (1.0 - decay_rate) * (
        stats[0:1] * (1.0 / width) + tiny_square
    )
    mean_row = pick(0) * (1.0 / width)
    update_total = mean_row * jnp.sum(stats[1:2] / cols, axis=1, keepdims=True)
    update_rms = jnp.sqrt(update_total * (1.0 / (width * hidden)))
    weight_rms = jnp.sqrt(pick(1) * (1.0 / (width * hidden)))
    factor = (
        jnp.sqrt(mean_row)
        * jnp.maximum(weight_floor, weight_rms)
        / jnp.maximum(1.0, update_rms / clip_level)
    )
    inv = factor * lax.rsqrt(cols)
    cols_new[...], inv_cols[...] = cols, inv
    for z in range(ZH):
        near, far = [
            (v[z, :, :hidden] - learn_rate * (v[z, :, hidden:] * inv)).astype(bf16)
            for v in (near_half, far_half)
        ]
        a_half[z] = jnp.where(upper, far, near)
        b_half[z] = jnp.where(upper, near, far)


def return_kernel(pos, near, far, weight, moment, inv_cols, new_weight, delta, rows_new):
    for k, source in enumerate((near, far)):
        rows = pl.ds(pl.multiple_of(GR * (k ^ pos[4]), GR), GR)
        g = source[...]
        moments = row_moment_of(moment[rows], g * g)
        change = g * lax.rsqrt(moments) * inv_cols[...]
        rows_new[rows] = moments
        delta[rows] = change
        new_weight[rows] = weight[rows] - learn_rate * change


def xor_perm(n, k):
    return [(d, d ^ k) for d in range(n)]


def exchange(pieces, axes):
    return [lax.ppermute(pieces[k], axes, xor_perm(4, k)) for k in (1, 2, 3)]


def four_sum(own, got):
    return (own + got[1]) + (got[0] + got[2])


def on_device(tokens, cotangent, weight, row_moment, col_moment):
    tok_rows, width = tokens.shape
    hidden = cotangent.shape[1]
    seg = width // 16
    cuts, y1, y0, xlo, z, core = [lax.axis_index(a) for a in AXES]
    pos = jnp.stack([core, y1, y0, xlo, cuts, reverse_bits(z)]).astype(jnp.int32)
    params = pltpu.CompilerParams(vmem_limit_bytes=16 * 2**20)
    small = pltpu.CompilerParams(vmem_limit_bytes=6 * 2**20)
    cost = pl.CostEstimate(
        flops=64 * tok_rows * seg * hidden, bytes_accessed=16 * 2**20, transcendentals=0
    )
    piece = (2, 2, ZH, GR, hidden)
    whole = pl.BlockSpec((tok_rows, hidden), lambda g, pos: (0, 0))
    piece_spec = pl.BlockSpec((1,) + piece[1:], lambda g, pos: (g, 0, 0, 0, 0))

    def tok_specs(part, step):
        index = cols_at(part, step)
        return [
            pl.BlockSpec((tok_rows, seg), lambda g, pos: (0, pos[0] * 8 + index(g, pos))),
            pl.BlockSpec((tok_rows, seg), lambda g, pos: (0, g)),
        ]

    order = [(0, 1), (1, 1), (0, 0), (1, 0)]
    cotangent2 = lax.ppermute(cotangent, "core", SWAP)
    tokens2 = {}
    for part, step in order:
        index = cols_at(part, step)
        away_cols = pl.pallas_call(
            copy_kernel,
            out_shape=jax.ShapeDtypeStruct((tok_rows, 2 * seg), tokens.dtype),
            grid_spec=pltpu.PrefetchScalarGridSpec(
                num_scalar_prefetch=1,
                grid=(2,),
                in_specs=[
                    pl.BlockSpec(
                        (tok_rows, seg),
                        lambda g, pos, index=index: (0, (1 - pos[0]) * 8 + index(g, pos)),
                    )
                ],
                out_specs=pl.BlockSpec((tok_rows, seg), lambda g, pos: (0, g)),
            ),
            compiler_params=small,
        )(pos, tokens)
        tokens2[part, step] = lax.ppermute(away_cols, "core", SWAP)

    in_specs = lambda n: [pl.BlockSpec(memory_space=pltpu.SMEM)] + [
        pl.BlockSpec(memory_space=pltpu.VMEM)
    ] * n
    moment = row_moment[:, None]
    packed = pl.pallas_call(
        pack_kernel,
        out_shape=jax.ShapeDtypeStruct((GR, hidden + 128), f32),
        in_specs=in_specs(2),
        compiler_params=small,
    )(pos, weight, moment)
    packed = lax.ppermute(packed, TURNED, TURN)

    parts = {}
    for part, step in order:
        kept = jax.ShapeDtypeStruct(piece, bf16 if step else f32)
        parts[part, step], parts[part, 2 + step] = pl.pallas_call(
            functools.partial(grad_kernel, part),
            out_shape=[kept, jax.ShapeDtypeStruct(piece, bf16)],
            grid_spec=pltpu.PrefetchScalarGridSpec(
                num_scalar_prefetch=1,
                grid=(2,),
                in_specs=tok_specs(part, step) + [whole] * 2,
                out_specs=[piece_spec] * 2,
            ),
            compiler_params=params,
            cost_estimate=cost,
        )(pos, tokens, tokens2[part, step], cotangent, cotangent2)
    a_parts, b_parts = [[parts[p, k] for k in range(4)] for p in range(2)]
    a_got, b_got = exchange(a_parts, Y), exchange(b_parts, X)
    a_sum = a_parts[0] + sum(p.astype(f32) for p in a_got)
    b_sum = b_parts[0] + sum(p.astype(f32) for p in b_got)

    a_parts = [a_sum[k % 2, k // 2] for k in range(4)]
    b_parts = [b_sum[k % 2, k // 2] for k in range(4)]
    a_got = exchange([p.astype(bf16) for p in a_parts], X)
    b_got = exchange([p.astype(bf16) for p in b_parts], Y)
    b_got, packed = lax.optimization_barrier((b_got, packed))
    line, part_line, block = (ZN, GR, hidden), (ZH, GR, hidden), (GR, hidden)
    keep, send = pl.pallas_call(
        second_sum_kernel,
        out_shape=[jax.ShapeDtypeStruct(part_line, f32), jax.ShapeDtypeStruct(part_line, bf16)],
        in_specs=in_specs(8),
        compiler_params=small,
    )(pos, a_parts[0], *a_got, b_parts[0], *b_got)

    got = lax.ppermute(send, "z", xor_perm(ZN, 1))
    blocks = pl.pallas_call(
        third_sum_kernel,
        out_shape=[jax.ShapeDtypeStruct(block, f32)] + [jax.ShapeDtypeStruct(block, bf16)] * 3,
        in_specs=in_specs(2),
        compiler_params=small,
    )(pos, keep, got)
    got = [lax.ppermute(blocks[k], "z", xor_perm(ZN, LINE_STEP[k])) for k in (1, 2, 3)]
    g32 = blocks[0] + sum(p.astype(f32) for p in got)

    near = lax.ppermute(g32, TURNED, TURN)
    far = lax.ppermute(g32, ("cuts",) + TURNED, FAR_TURN)

    stats, own = pl.pallas_call(
        stats_kernel,
        out_shape=[
            jax.ShapeDtypeStruct((8, hidden), f32),
            jax.ShapeDtypeStruct((GR, 2 * hidden), f32),
        ],
        compiler_params=small,
    )(g32, packed)
    got = [lax.ppermute(own, "z", xor_perm(ZN, LINE_STEP[k])) for k in (1, 2, 3)]
    near_half = pl.pallas_call(
        line_kernel,
        out_shape=jax.ShapeDtypeStruct((ZH,) + own.shape, f32),
        in_specs=in_specs(4),
        compiler_params=small,
    )(pos, own, *got)
    far_half = lax.ppermute(near_half, "z", xor_perm(ZN, 1))
    stats = stats + lax.ppermute(stats, "core", SWAP)
    stats = four_sum(stats, exchange([stats] * 4, Y))
    stats = four_sum(stats, exchange([stats] * 4, X))
    stats = four_sum(stats, [lax.ppermute(stats, "z", xor_perm(ZN, k)) for k in (1, 2, 3)])
    stats = stats + lax.ppermute(stats, "z", xor_perm(ZN, 4))
    stats, near, far = lax.optimization_barrier((stats, near, far))

    row_vector = jax.ShapeDtypeStruct((1, hidden), f32)
    a_half, b_half, cols_new, inv_cols = pl.pallas_call(
        functools.partial(rows_kernel, width),
        out_shape=[jax.ShapeDtypeStruct((ZH, GR, hidden), bf16)] * 2 + [row_vector] * 2,
        in_specs=in_specs(4),
        compiler_params=small,
    )(pos, stats, col_moment.reshape(1, hidden), near_half, far_half)
    a_all = [a_half] + exchange([a_half] * 4, X)
    b_all = [b_half] + exchange([b_half] * 4, Y)
    a_half = jnp.stack([a_all[0], a_all[2], a_all[1], a_all[3]]).reshape(piece)
    b_half = jnp.stack([b_all[0], b_all[2], b_all[1], b_all[3]]).reshape(piece)
    slab = jax.ShapeDtypeStruct(weight.shape, f32)
    new_weight, delta, rows_new = pl.pallas_call(
        return_kernel,
        out_shape=[slab, slab, jax.ShapeDtypeStruct((weight.shape[0], 1), f32)],
        in_specs=in_specs(5),
        compiler_params=small,
    )(pos, near, far, weight, moment, inv_cols)
    a_half, b_half, rows_new = lax.optimization_barrier((a_half, b_half, rows_new))
    a_all, b_all = [a_half], [b_half]
    got = {}
    for k in (2, 1, 3):
        got[0, k] = lax.ppermute(a_half, Y, xor_perm(4, k))
        got[1, k] = lax.ppermute(b_half, X, xor_perm(4, k))
    a_all += [got[0, k] for k in (1, 2, 3)]
    b_all += [got[1, k] for k in (1, 2, 3)]

    result = jax.ShapeDtypeStruct((tok_rows, hidden), f32)
    sums = []
    for part, step in [(0, 0), (1, 0), (0, 1), (1, 1)]:
        halves = (a_all, b_all)[part]
        sums = pl.pallas_call(
            functools.partial(apply_kernel, part),
            out_shape=[result, result],
            grid_spec=pltpu.PrefetchScalarGridSpec(
                num_scalar_prefetch=1,
                grid=(2,),
                in_specs=tok_specs(part, step)
                + [piece_spec] * 2
                + [whole] * len(sums),
                out_specs=[whole] * 2,
                scratch_shapes=[pltpu.VMEM((ZH, 2, 2, GR, hidden), bf16)],
            ),
            compiler_params=params,
            cost_estimate=cost,
        )(pos, tokens, tokens2[part, step], halves[step], halves[2 + step], *sums)
    own, away = sums
    summed = own + lax.ppermute(away, "core", SWAP)
    preact = (summed * (1.0 / math.sqrt(width))).astype(bf16)
    return (new_weight, delta, rows_new[:, 0], cols_new[0], preact)


def solution(mesh):
    fine = Mesh(mesh.devices.reshape(SIZES), AXES)
    fsdp = ("y1", "y0", "xlo", "z", "core")
    rows = P(("cuts",) + fsdp, None)
    return jax.shard_map(
        on_device,
        mesh=fine,
        in_specs=(rows, rows, P(fsdp, None), P(fsdp), P()),
        out_specs=(P(fsdp, None), P(fsdp, None), P(fsdp), P(), rows),
        check_vma=False,
    )
```

```python
import functools
import math

import jax
import jax.numpy as jnp
from jax import lax
from jax.experimental import pallas as pl
from jax.experimental.pallas import tpu as pltpu
from jax.sharding import Mesh, PartitionSpec as P

decay_rate = 0.9
tiny_square = 1e-30
clip_level = 1.0
weight_floor = 0.001
learn_rate = 0.1

f32 = jnp.float32
bf16 = jnp.bfloat16

AXES = ("cuts", "y1", "y0", "xlo", "z", "core")
SIZES = (2, 2, 2, 2, 8, 2)
Y = ("y1", "y0")
X = ("cuts", "xlo")
ZN = 8
ZH = 4
GR = 32
SWAP = [(0, 1), (1, 0)]


def reverse_bits(z):
    return (z & 1) * 4 + (z & 2) + ((z >> 2) & 1)


TURN = [
    ((y * ZN + z) * 2 + c, (c * ZN + reverse_bits(z)) * 2 + y)
    for y in range(2)
    for z in range(ZN)
    for c in range(2)
]
FAR_TURN = [(d + 32 * q, e + 32 * (1 - q)) for q in range(2) for d, e in TURN]
TURNED = ("y1", "z", "core")
LINE_STEP = {1: 4, 2: 2, 3: 6}


def cols_at(part, step):
    def index(g, pos):
        row_bit, x_bit = (step, g) if part == 0 else (g, step)
        return (pos[2] ^ row_bit) * 4 + (pos[3] ^ x_bit) * 2 + part

    return index


def chosen(pos, part):
    return (pos[1], pos[4]) if part == 0 else (pos[4], pos[1])


def pack_kernel(pos, weight, moment, out):
    rows = pl.ds(pl.multiple_of(GR * pos[4], GR), GR)
    hidden = weight.shape[-1]
    out[:, :hidden] = weight[rows]
    out[:, hidden:] = jnp.broadcast_to(moment[rows], (GR, out.shape[-1] - hidden))


def copy_kernel(pos, src, dst):
    dst[...] = src[...]


def grad_kernel(part, pos, tok, tok2, cot, cot2, out0, out1):
    pick, inner = chosen(pos, part)
    dims = (((0,), (0,)), ((), ()))
    g = lax.dot_general(tok[...], cot[...], dims, preferred_element_type=f32)
    g = g + lax.dot_general(tok2[...], cot2[...], dims, preferred_element_type=f32)
    g = g.reshape(ZH, 2, 2, GR, g.shape[-1])
    for k in range(2):
        first, second = (g[:, 0, k], g[:, 1, k]) if part == 0 else (g[:, k, 0], g[:, k, 1])
        out0[0, k ^ inner] = jnp.where(pick == 0, first, second).astype(out0.dtype)
        out1[0, k ^ inner] = jnp.where(pick == 0, second, first).astype(out1.dtype)


def apply_kernel(part, pos, tok, tok2, piece0, piece1, *refs):
    sums, (own, away, half) = refs[:-3], refs[-3:]
    pick, inner = chosen(pos, part)
    for k in range(2):
        zero, one = piece0[0, k ^ inner], piece1[0, k ^ inner]
        first, second = jnp.where(pick == 0, zero, one), jnp.where(pick == 0, one, zero)
        if part == 0:
            half[:, 0, k], half[:, 1, k] = first, second
        else:
            half[:, k, 0], half[:, k, 1] = first, second
    h = half[...].reshape(-1, half.shape[-1])

    @pl.when(pl.program_id(0) == 0)
    def _():
        for out, begin in zip((own, away), sums or (None, None)):
            out[...] = jnp.zeros_like(out) if begin is None else begin[...]

    own[...] += jnp.dot(tok[...], h, preferred_element_type=f32)
    away[...] += jnp.dot(tok2[...], h, preferred_element_type=f32)


def second_sum_kernel(pos, *refs):
    ins, (keep, send) = refs[:8], refs[8:]
    a_sum, b_sum = [
        ins[n][...] + sum(ins[n + k][...].astype(f32) for k in (1, 2, 3)) for n in (0, 4)
    ]
    upper = pos[5] >= ZH
    keep[...] = jnp.where(upper, b_sum, a_sum)
    send[...] = jnp.where(upper, a_sum, b_sum).astype(bf16)


def third_sum_kernel(pos, keep, got, *outs):
    for k in range(4):
        block = (pos[5] % ZH) ^ k
        outs[k][...] = (keep[block] + got[block].astype(f32)).astype(outs[k].dtype)


def line_kernel(pos, *refs):
    for k in range(4):
        refs[4][(pos[5] % ZH) ^ k] = refs[k][...]


def row_moment_of(moment, squares):
    mean = jnp.sum(squares, axis=1, keepdims=True) * (1.0 / squares.shape[1])
    return decay_rate * moment + (1.0 - decay_rate) * (mean + tiny_square)


def stats_kernel(g32, packed, stats, block):
    hidden = g32.shape[-1]
    g, w = g32[...], packed[:, :hidden]
    squares = g * g
    rows = row_moment_of(packed[:, hidden : hidden + 1], squares)
    u = g * lax.rsqrt(rows)
    block[:, :hidden], block[:, hidden:] = w, u
    lane = lax.broadcasted_iota(jnp.int32, (1, hidden), 1)
    total = lambda v: jnp.sum(v, axis=0, keepdims=True)
    scalars = jnp.where(lane == 0, total(rows), 0.0) + jnp.where(
        lane == 1, jnp.sum(total(w * w), axis=1, keepdims=True), 0.0
    )
    stats[...] = jnp.zeros_like(stats)
    stats[0:1], stats[1:2], stats[2:3] = total(squares), total(u * u), scalars


def rows_kernel(width, pos, stats, col_moment, near_half, far_half, *outs):
    a_half, b_half, cols_new, inv_cols = outs
    hidden = stats.shape[-1]
    upper = pos[5] >= ZH
    lane = lax.broadcasted_iota(jnp.int32, (1, hidden), 1)
    pick = lambda k: jnp.sum(jnp.where(lane == k, stats[2:3], 0.0), axis=1, keepdims=True)
    cols = decay_rate * col_moment[...] + (1.0 - decay_rate) * (
        stats[0:1] * (1.0 / width) + tiny_square
    )
    mean_row = pick(0) * (1.0 / width)
    update_total = mean_row * jnp.sum(stats[1:2] / cols, axis=1, keepdims=True)
    update_rms = jnp.sqrt(update_total * (1.0 / (width * hidden)))
    weight_rms = jnp.sqrt(pick(1) * (1.0 / (width * hidden)))
    factor = (
        jnp.sqrt(mean_row)
        * jnp.maximum(weight_floor, weight_rms)
        / jnp.maximum(1.0, update_rms / clip_level)
    )
    inv = factor * lax.rsqrt(cols)
    cols_new[...], inv_cols[...] = cols, inv
    for z in range(ZH):
        near, far = [
            (v[z, :, :hidden] - learn_rate * (v[z, :, hidden:] * inv)).astype(bf16)
            for v in (near_half, far_half)
        ]
        a_half[z] = jnp.where(upper, far, near)
        b_half[z] = jnp.where(upper, near, far)


def return_kernel(pos, near, far, weight, moment, inv_cols, new_weight, delta, rows_new):
    for k, source in enumerate((near, far)):
        rows = pl.ds(pl.multiple_of(GR * (k ^ pos[4]), GR), GR)
        g = source[...]
        moments = row_moment_of(moment[rows], g * g)
        change = g * lax.rsqrt(moments) * inv_cols[...]
        rows_new[rows] = moments
        delta[rows] = change
        new_weight[rows] = weight[rows] - learn_rate * change


def xor_perm(n, k):
    return [(d, d ^ k) for d in range(n)]


def exchange(pieces, axes):
    return [lax.ppermute(pieces[k], axes, xor_perm(4, k)) for k in (1, 2, 3)]


def four_sum(own, got):
    return (own + got[1]) + (got[0] + got[2])


def on_device(tokens, cotangent, weight, row_moment, col_moment):
    tok_rows, width = tokens.shape
    hidden = cotangent.shape[1]
    seg = width // 16
    cuts, y1, y0, xlo, z, core = [lax.axis_index(a) for a in AXES]
    pos = jnp.stack([core, y1, y0, xlo, cuts, reverse_bits(z)]).astype(jnp.int32)
    params = pltpu.CompilerParams(vmem_limit_bytes=32 * 2**20)
    small = pltpu.CompilerParams(vmem_limit_bytes=32 * 2**20)
    cost = pl.CostEstimate(
        flops=64 * tok_rows * seg * hidden, bytes_accessed=16 * 2**20, transcendentals=0
    )
    piece = (2, 2, ZH, GR, hidden)
    whole = pl.BlockSpec((tok_rows, hidden), lambda g, pos: (0, 0))
    piece_spec = pl.BlockSpec((1,) + piece[1:], lambda g, pos: (g, 0, 0, 0, 0))

    def tok_specs(part, step):
        index = cols_at(part, step)
        return [
            pl.BlockSpec((tok_rows, seg), lambda g, pos: (0, pos[0] * 8 + index(g, pos))),
            pl.BlockSpec((tok_rows, seg), lambda g, pos: (0, g)),
        ]

    order = [(0, 1), (1, 1), (0, 0), (1, 0)]
    cotangent2 = lax.ppermute(cotangent, "core", SWAP)
    tokens2 = {}
    for part, step in order:
        index = cols_at(part, step)
        away_cols = pl.pallas_call(
            copy_kernel,
            out_shape=jax.ShapeDtypeStruct((tok_rows, 2 * seg), tokens.dtype),
            grid_spec=pltpu.PrefetchScalarGridSpec(
                num_scalar_prefetch=1,
                grid=(2,),
                in_specs=[
                    pl.BlockSpec(
                        (tok_rows, seg),
                        lambda g, pos, index=index: (0, (1 - pos[0]) * 8 + index(g, pos)),
                    )
                ],
                out_specs=pl.BlockSpec((tok_rows, seg), lambda g, pos: (0, g)),
            ),
            compiler_params=small,
        )(pos, tokens)
        tokens2[part, step] = lax.ppermute(away_cols, "core", SWAP)

    in_specs = lambda n: [pl.BlockSpec(memory_space=pltpu.SMEM)] + [
        pl.BlockSpec(memory_space=pltpu.VMEM)
    ] * n
    moment = row_moment[:, None]
    packed = pl.pallas_call(
        pack_kernel,
        out_shape=jax.ShapeDtypeStruct((GR, hidden + 128), f32),
        in_specs=in_specs(2),
        compiler_params=small,
    )(pos, weight, moment)
    packed = lax.ppermute(packed, TURNED, TURN)

    parts = {}
    for part, step in order:
        kept = jax.ShapeDtypeStruct(piece, bf16 if step else f32)
        parts[part, step], parts[part, 2 + step] = pl.pallas_call(
            functools.partial(grad_kernel, part),
            out_shape=[kept, jax.ShapeDtypeStruct(piece, bf16)],
            grid_spec=pltpu.PrefetchScalarGridSpec(
                num_scalar_prefetch=1,
                grid=(2,),
                in_specs=tok_specs(part, step) + [whole] * 2,
                out_specs=[piece_spec] * 2,
            ),
            compiler_params=params,
            cost_estimate=cost,
        )(pos, tokens, tokens2[part, step], cotangent, cotangent2)
    a_parts, b_parts = [[parts[p, k] for k in range(4)] for p in range(2)]
    a_got, b_got = exchange(a_parts, Y), exchange(b_parts, X)
    a_sum = a_parts[0] + sum(p.astype(f32) for p in a_got)
    b_sum = b_parts[0] + sum(p.astype(f32) for p in b_got)

    a_parts = [a_sum[k % 2, k // 2] for k in range(4)]
    b_parts = [b_sum[k % 2, k // 2] for k in range(4)]
    a_got = exchange([p.astype(bf16) for p in a_parts], X)
    b_got = exchange([p.astype(bf16) for p in b_parts], Y)
    b_got, packed = lax.optimization_barrier((b_got, packed))
    line, part_line, block = (ZN, GR, hidden), (ZH, GR, hidden), (GR, hidden)
    keep, send = pl.pallas_call(
        second_sum_kernel,
        out_shape=[jax.ShapeDtypeStruct(part_line, f32), jax.ShapeDtypeStruct(part_line, bf16)],
        in_specs=in_specs(8),
        compiler_params=small,
    )(pos, a_parts[0], *a_got, b_parts[0], *b_got)

    got = lax.ppermute(send, "z", xor_perm(ZN, 1))
    blocks = pl.pallas_call(
        third_sum_kernel,
        out_shape=[jax.ShapeDtypeStruct(block, f32)] + [jax.ShapeDtypeStruct(block, bf16)] * 3,
        in_specs=in_specs(2),
        compiler_params=small,
    )(pos, keep, got)
    got = [lax.ppermute(blocks[k], "z", xor_perm(ZN, LINE_STEP[k])) for k in (1, 2, 3)]
    g32 = blocks[0] + sum(p.astype(f32) for p in got)

    near = lax.ppermute(g32, TURNED, TURN)
    far = lax.ppermute(g32, ("cuts",) + TURNED, FAR_TURN)

    stats, own = pl.pallas_call(
        stats_kernel,
        out_shape=[
            jax.ShapeDtypeStruct((8, hidden), f32),
            jax.ShapeDtypeStruct((GR, 2 * hidden), f32),
        ],
        compiler_params=small,
    )(g32, packed)
    got = [lax.ppermute(own, "z", xor_perm(ZN, LINE_STEP[k])) for k in (1, 2, 3)]
    near_half = pl.pallas_call(
        line_kernel,
        out_shape=jax.ShapeDtypeStruct((ZH,) + own.shape, f32),
        in_specs=in_specs(4),
        compiler_params=small,
    )(pos, own, *got)
    far_half = lax.ppermute(near_half, "z", xor_perm(ZN, 1))
    stats = stats + lax.ppermute(stats, "core", SWAP)
    stats = four_sum(stats, exchange([stats] * 4, Y))
    stats = four_sum(stats, exchange([stats] * 4, X))
    stats = four_sum(stats, [lax.ppermute(stats, "z", xor_perm(ZN, k)) for k in (1, 2, 3)])
    stats = stats + lax.ppermute(stats, "z", xor_perm(ZN, 4))
    stats, near, far = lax.optimization_barrier((stats, near, far))

    row_vector = jax.ShapeDtypeStruct((1, hidden), f32)
    a_half, b_half, cols_new, inv_cols = pl.pallas_call(
        functools.partial(rows_kernel, width),
        out_shape=[jax.ShapeDtypeStruct((ZH, GR, hidden), bf16)] * 2 + [row_vector] * 2,
        in_specs=in_specs(4),
        compiler_params=small,
    )(pos, stats, col_moment.reshape(1, hidden), near_half, far_half)
    a_all = [a_half] + exchange([a_half] * 4, X)
    b_all = [b_half] + exchange([b_half] * 4, Y)
    a_half = jnp.stack([a_all[0], a_all[2], a_all[1], a_all[3]]).reshape(piece)
    b_half = jnp.stack([b_all[0], b_all[2], b_all[1], b_all[3]]).reshape(piece)
    slab = jax.ShapeDtypeStruct(weight.shape, f32)
    new_weight, delta, rows_new = pl.pallas_call(
        return_kernel,
        out_shape=[slab, slab, jax.ShapeDtypeStruct((weight.shape[0], 1), f32)],
        in_specs=in_specs(5),
        compiler_params=small,
    )(pos, near, far, weight, moment, inv_cols)
    a_half, b_half, rows_new = lax.optimization_barrier((a_half, b_half, rows_new))
    a_all, b_all = [a_half], [b_half]
    got = {}
    for k in (2, 1, 3):
        got[0, k] = lax.ppermute(a_half, Y, xor_perm(4, k))
        got[1, k] = lax.ppermute(b_half, X, xor_perm(4, k))
    a_all += [got[0, k] for k in (1, 2, 3)]
    b_all += [got[1, k] for k in (1, 2, 3)]

    result = jax.ShapeDtypeStruct((tok_rows, hidden), f32)
    sums = []
    for part, step in [(0, 0), (1, 0), (0, 1), (1, 1)]:
        halves = (a_all, b_all)[part]
        sums = pl.pallas_call(
            functools.partial(apply_kernel, part),
            out_shape=[result, result],
            grid_spec=pltpu.PrefetchScalarGridSpec(
                num_scalar_prefetch=1,
                grid=(2,),
                in_specs=tok_specs(part, step)
                + [piece_spec] * 2
                + [whole] * len(sums),
                out_specs=[whole] * 2,
                scratch_shapes=[pltpu.VMEM((ZH, 2, 2, GR, hidden), bf16)],
            ),
            compiler_params=params,
            cost_estimate=cost,
        )(pos, tokens, tokens2[part, step], halves[step], halves[2 + step], *sums)
    own, away = sums
    summed = own + lax.ppermute(away, "core", SWAP)
    preact = (summed * (1.0 / math.sqrt(width))).astype(bf16)
    return (new_weight, delta, rows_new[:, 0], cols_new[0], preact)


def solution(mesh):
    fine = Mesh(mesh.devices.reshape(SIZES), AXES)
    fsdp = ("y1", "y0", "xlo", "z", "core")
    rows = P(("cuts",) + fsdp, None)
    return jax.shard_map(
        on_device,
        mesh=fine,
        in_specs=(rows, rows, P(fsdp, None), P(fsdp), P()),
        out_specs=(P(fsdp, None), P(fsdp, None), P(fsdp), P(), rows),
        check_vma=False,
    )
```
